32 devices in a mesh: groups: 2 (over x), layer: 8 (over z, y), loop: 2 (over core).
Axes of the slice: x: 2, y: 2, z: 4, core: 2. Of those that a mesh axis runs over, the one named last changes fastest.
Arguments:
- acts: bfloat16 [8, 1536, 2048], P('layer', ('groups', 'loop')), parts along dimension 1, may hold values from -6 to 6
- grads: bfloat16 [8, 1536, 7168], P('layer', ('groups', 'loop')), parts along dimension 1, may hold values from -6 to 6
- act_factors: bfloat16 [8, 2048, 512], P('layer', None, 'loop'), may hold values from -0.0008544922 to 0.0008544922
- grad_factors: bfloat16 [8, 7168, 512], P('layer', None, 'loop'), may hold values from -0.03125 to 0.03125
- lengths: int32 [16], P(('groups', 'loop')), parts along dimension 0, may hold values from 1 to 96, 480 in all
Outputs:
- scores: float32 [16, 16], P('groups'), parts along dimension 0
The draws below stay inside these ranges and needn't reach their ends.
There are 2 independent parts, one for each index of `groups`. The reference program is written for one: setup_inputs(seed, part) draws one part's arguments, and reference() takes and returns one part's arrays. A program takes and returns all parts, laid end to end along the dimension named above; an argument that names none is the same for every part. Nothing has to cross between parts.
Inputs may be any that keep to these rules, and one draw needn't show every extreme that they name: The lengths of one group sum to 480, and the largest is 96.
All inputs are finite; a program needn't handle non-finite values.
Results may differ from the reference program's by a relative error of at most 0.0003.
Values may be sent and summed in bfloat16 or wider, within the bound.
No kernel may reach another device: no remote copies, remote signals or barrier semaphores. Data moves between devices by JAX's collectives and lax.ppermute only.
A program may use at most 64 MiB of HBM per device.

```python
import math
import jax
import jax.numpy as jnp
import numpy as np

D = 8192
FF = 28672
RANK = 32
PAD = 96
SEQS = 8
TOKENS = 768
QUERIES = 16
LAYERS = 2
N_LAYER = 8


def steps_of(own_key, extent, split, smallest, high):
    def one(position, blocks):
        heights = jax.random.uniform(jax.random.fold_in(jax.random.fold_in(own_key, 6), position), (blocks,), jnp.float32, smallest / len(split), high / len(split))
        return jnp.repeat(jnp.exp(heights), extent[position] // blocks).reshape((-1,) + (1,) * (len(extent) - position - 1))

    gain = one(*split[0])
    for cut in split[1:]:
        gain = gain * one(*cut)
    return gain


def length_profile(amount, total, reach, slope):
    loads = [(1 << 20) // math.isqrt(standing ** slope) + 1 for standing in range(2, amount + 1)]
    surplus, counts = total - reach - (amount - 1), [1] * (amount - 1)
    while surplus > 0:
        movable = [i for i in range(amount - 1) if counts[i] < reach]
        whole, left = sum([loads[i] for i in movable]), surplus
        for i in movable:
            more = min(reach - counts[i], max(1, left * loads[i] // whole), surplus)
            counts[i] = counts[i] + more
            surplus = surplus - more
    return np.array([reach] + counts)


def ragged_sizes(own_key, number_of, total, limit, slope):
    if number_of == 2:
        one = jax.random.randint(own_key, (), max(1, total - limit), min(limit, total - 1) + 1)
        return jnp.stack([one, total - one])
    sizes = jnp.asarray(length_profile(number_of, total, limit, slope), jnp.int32)
    pairs = (number_of - 1) // 2
    giver, sink = sizes[1:1 + 2 * pairs:2], sizes[2:2 + 2 * pairs:2]
    room = jnp.minimum(giver - 1, limit - sink)
    moved = jax.random.randint(jax.random.fold_in(own_key, 1), (pairs,), 0, 1 << 20) % (room + 1)
    sizes = sizes.at[1:1 + 2 * pairs:2].set(giver - moved).at[2:2 + 2 * pairs:2].set(sink + moved)
    return sizes[jax.random.permutation(jax.random.fold_in(own_key, 2), number_of)]


def centred(key, extent, spread, limit, cuts=(), kind=jnp.bfloat16):
    entries = spread * jax.random.normal(key, extent, jnp.float32)
    if cuts:
        entries = entries * steps_of(key, extent, cuts, -0.22, 0.18)
    return jnp.clip(entries, -limit, limit).astype(kind)


def setup_inputs(seed: int = 0, part: int = 0) -> dict:
    key_of = jax.random.split(jax.random.key(seed), 6)
    part_splits = jax.random.split(jax.random.fold_in(key_of[5], part), 6)
    return {
        "acts": centred(part_splits[0], (N_LAYER, TOKENS, D // 4), 1.0, 6.0, ((0, 8), (1, 2))),
        "grads": centred(part_splits[1], (N_LAYER, TOKENS, FF // 4), 1.0, 6.0, ((0, 8), (1, 2))),
        "act_factors": centred(key_of[2], (N_LAYER, D // 4, QUERIES * RANK), (D * RANK * PAD * LAYERS) ** -0.5, 0.0008544922, ((0, 8), (2, 2))),
        "grad_factors": centred(key_of[3], (N_LAYER, FF // 4, QUERIES * RANK), FF ** -0.5, 0.03125, ((0, 8), (2, 2))),
        "lengths": ragged_sizes(part_splits[4], SEQS, SEQS * PAD * 5 // 8, PAD, 1).astype(jnp.int32),
    }


def reference(acts, grads, act_factors, grad_factors, lengths):
    positions = jnp.arange(PAD, dtype=jnp.int32)
    valid_mask = (positions[None, :] < lengths[:, None]).astype(jnp.float32).reshape(TOKENS)
    score_total = jnp.zeros((SEQS, QUERIES), jnp.float32)
    for layer_index in range(N_LAYER // 4):
        lower = 4 * layer_index
        rows_act = jnp.concatenate([acts[lower + k] for k in range(4)], axis=1)
        rows_grad = jnp.concatenate([grads[lower + k] for k in range(4)], axis=1)
        factor_act = jnp.concatenate([act_factors[lower + k] for k in range(4)], axis=0)
        factor_grad = jnp.concatenate([grad_factors[lower + k] for k in range(4)], axis=0)
        act_proj = jnp.dot(rows_act, factor_act, preferred_element_type=jnp.float32)
        grad_proj = jnp.dot(rows_grad, factor_grad, preferred_element_type=jnp.float32)
        token_score = jnp.sum((act_proj * grad_proj).reshape(TOKENS, QUERIES, RANK), axis=2)
        token_score = token_score * valid_mask[:, None]
        score_total = score_total + jnp.sum(token_score.reshape(SEQS, PAD, QUERIES), axis=1)
    return score_total
```

```python
import jax
import jax.numpy as jnp
from jax import lax
from jax.sharding import PartitionSpec as P

RANK = 32
QUARTERS = 4


def from_partner(value, axis, mask):
    pairs = [(source, source ^ mask) for source in range(lax.axis_size(axis))]
    return lax.ppermute(value, axis, pairs)


def project(rows, factor):
    return jnp.dot(rows, factor, preferred_element_type=jnp.float32)


def sum_over_quarters(projected, quarter):
    parts = projected.reshape(QUARTERS, -1, projected.shape[1])
    total = lax.dynamic_index_in_dim(parts, quarter, 0, keepdims=False)
    for mask in range(1, QUARTERS):
        out = lax.dynamic_index_in_dim(parts, quarter ^ mask, 0, keepdims=False)
        total = total + from_partner(out, "layer", mask)
    return total


def on_device(acts, grads, act_factors, grad_factors, lengths):
    loop_count = lax.axis_size("loop")
    position = lax.axis_index("loop")
    layer_count = lax.axis_size("layer")
    quarter = lax.axis_index("layer") % QUARTERS
    seq_dev = lengths.shape[0]
    pad_rows = acts.shape[1] // seq_dev
    seq_part = seq_dev // QUARTERS
    other_grad = from_partner(grad_factors[0], "loop", 1)
    other_act = from_partner(act_factors[0], "loop", 1)
    mine = jnp.concatenate(
        [project(acts[0], act_factors[0]), project(grads[0], grad_factors[0])], axis=1
    )
    mine = sum_over_quarters(mine, quarter)
    other = jnp.concatenate(
        [project(acts[0], other_act), project(grads[0], other_grad)], axis=1
    )
    other = sum_over_quarters(other, quarter)
    my_lengths = lax.dynamic_slice_in_dim(lengths, quarter * seq_part, seq_part)
    offsets = jnp.arange(pad_rows, dtype=jnp.int32)
    live = (offsets[None, :] < my_lengths[:, None])[:, :, None]

    def score(both):
        act, grad = jnp.split(both, 2, axis=1)
        pair = jnp.where(live, (act * grad).reshape(seq_part, pad_rows, -1), 0)
        return jnp.sum(pair.reshape(seq_part, pad_rows, -1, RANK), axis=(1, 3))

    mine, other = score(mine), score(other)
    first = jnp.where(position == 0, mine, other)
    second = jnp.where(position == 0, other, mine)
    scores = jnp.concatenate([first, second], axis=1)
    total = jnp.zeros((seq_dev * loop_count, scores.shape[1]), jnp.float32)
    total = lax.dynamic_update_slice(
        total, scores, (position * seq_dev + quarter * seq_part, 0)
    )
    total = total + from_partner(total, "loop", 1)
    gathered = [from_partner(total, "layer", mask) for mask in range(1, QUARTERS)]
    total = total + gathered[0] + gathered[1] + gathered[2]
    mask = QUARTERS
    while mask < layer_count:
        total = total + from_partner(total, "layer", mask)
        mask *= 2
    return total


def solution(mesh):
    in_specs = (
        P("layer", ("groups", "loop"), None),
        P("layer", ("groups", "loop"), None),
        P("layer", None, "loop"),
        P("layer", None, "loop"),
        P(("groups", "loop")),
    )
    out_specs = P("groups", None)
    return jax.shard_map(
        on_device, mesh=mesh, in_specs=in_specs, out_specs=out_specs, check_vma=False
    )
```

```python
import functools

import jax
import jax.numpy as jnp
from jax import lax
from jax.experimental import pallas as pl
from jax.experimental.pallas import tpu as pltpu
from jax.sharding import PartitionSpec as P

RANK = 32
QUARTERS = 4
LANES = 128
CODE_ROWS = 16
TOP = 32000.0
STEPS = 256.0
FLOOR = 2.0**-112
CHUNK = 1024
MIB = 2**20

IN_VMEM = pl.BlockSpec(memory_space=pltpu.VMEM)
IN_HBM = pl.BlockSpec(memory_space=pltpu.HBM)
IN_SMEM = pl.BlockSpec(memory_space=pltpu.SMEM)


def from_partner(value, axis, mask):
    pairs = [(source, source ^ mask) for source in range(lax.axis_size(axis))]
    return lax.ppermute(value, axis, pairs)


def dot(rows, factor):
    return jnp.dot(rows, factor, preferred_element_type=jnp.float32)


def encode(part):
    peak = jnp.max(jnp.abs(part), axis=0, keepdims=True)
    code = jnp.ceil(jnp.log2(jnp.maximum(peak, FLOOR)) * STEPS) + 1.0
    fixed = jnp.round(part * (TOP * jnp.exp2(code * (-1.0 / STEPS))))
    code = jnp.broadcast_to(code, (CODE_ROWS, part.shape[1]))
    return fixed.astype(jnp.int32).astype(jnp.int16), code.astype(jnp.int32).astype(jnp.int16)


def decode(message, rows):
    fixed = message[:rows, :].astype(jnp.int32).astype(jnp.float32)
    code = message[rows:, :].astype(jnp.int32).astype(jnp.float32)[:1]
    return fixed * (jnp.exp2(code * (1.0 / STEPS)) * (1.0 / TOP))


def share(total, quarter, own_ref, out_refs, first):
    rows = own_ref.shape[0]
    columns = slice(first, first + total.shape[2])
    own_ref[:, columns] = total[quarter]
    for mask in range(1, QUARTERS):
        fixed, code = encode(total[quarter ^ mask])
        out_refs[mask - 1][:rows, columns] = fixed
        out_refs[mask - 1][rows:, columns] = code


def own_kernel(place, acts, grads, act_factors, grad_factors,
               act_rows, grad_rows, own, out1, out2, out3,
               act_held, grad_held, total, act_sems, grad_sems):
    quarter = place[0]
    rows = own.shape[0]
    copies = []
    for source, rows_ref, factor, held, sems in (
        (acts, act_rows, act_factors, act_held, act_sems),
        (grads, grad_rows, grad_factors, grad_held, grad_sems),
    ):
        mine = []
        for step in range(source.shape[1] // CHUNK):
            depth = pl.ds(step * CHUNK, CHUNK)
            pair = (
                pltpu.make_async_copy(source.at[:, depth], rows_ref.at[:, depth], sems.at[0, step]),
                pltpu.make_async_copy(factor.at[depth, :], held.at[depth, :], sems.at[1, step]),
            )
            for copy in pair:
                copy.start()
            mine.append(pair)
        copies.append(mine)
    first = 0
    for mine, rows_ref, held in ((copies[0], act_rows, act_held), (copies[1], grad_rows, grad_held)):
        for step, pair in enumerate(mine):
            for copy in pair:
                copy.wait()
            depth = slice(step * CHUNK, (step + 1) * CHUNK)
            part = dot(rows_ref[:, depth], held[depth, :])
            for quarter_at in range(QUARTERS):
                block = part[quarter_at * rows:(quarter_at + 1) * rows]
                if step == 0:
                    total[quarter_at] = block
                else:
                    total[quarter_at] += block
        share(total, quarter, own, (out1, out2, out3), first)
        first += held.shape[1]


def other_kernel(place, act_rows, grad_rows, act_factors, grad_factors, own, out1, out2, out3, total):
    quarter = place[0]
    rows = own.shape[0]
    first = 0
    for rows_ref, factor in ((grad_rows, grad_factors), (act_rows, act_factors)):
        part = dot(rows_ref[...], factor[...])
        for quarter_at in range(QUARTERS):
            total[quarter_at] = part[quarter_at * rows:(quarter_at + 1) * rows]
        share(total, quarter, own, (out1, out2, out3), first)
        first += factor.shape[1]


def score_kernel(place, lengths, mine, mine1, mine2, mine3, other, other1, other2, other3, out):
    quarter, position = place[0], place[1]
    rows, width = mine.shape[0], mine.shape[1] // 2
    seq_part = lengths.shape[0] // QUARTERS
    pad_rows = rows // seq_part
    queries = width // RANK
    column = lax.broadcasted_iota(jnp.int32, (width, LANES), 0) // RANK
    lane = lax.broadcasted_iota(jnp.int32, (width, LANES), 1)
    offsets = lax.broadcasted_iota(jnp.int32, (pad_rows, width), 0)
    line = lax.broadcasted_iota(jnp.int32, out.shape, 0)
    result = jnp.zeros(out.shape, jnp.float32)
    units = (
        (mine, (mine1, mine2, mine3), position),
        (other, (other1, other2, other3), 1 - position),
    )
    for own, received, half in units:
        full = own[...]
        for message in received:
            full = full + decode(message[...], rows)
        pair = full[:, :width] * full[:, width:]
        pick = (lane == column + half * queries).astype(jnp.float32)
        for seq in range(seq_part):
            live = offsets < lengths[quarter * seq_part + seq]
            sums = jnp.sum(
                jnp.where(live, pair[seq * pad_rows:(seq + 1) * pad_rows], 0.0), axis=0, keepdims=True
            )
            sums = jnp.broadcast_to(sums, (8, width))
            scores = jnp.dot(
                sums, pick, precision=lax.Precision.HIGHEST, preferred_element_type=jnp.float32
            )[:1]
            at = (position * QUARTERS + quarter) * seq_part + seq
            result = result + jnp.where(line == at, scores, 0.0)
    out[...] = result


def on_device(acts, grads, act_factors, grad_factors, lengths):
    loop_count = lax.axis_size("loop")
    layer_count = lax.axis_size("layer")
    quarter = lax.axis_index("layer") % QUARTERS
    place = jnp.stack([quarter, lax.axis_index("loop")]).astype(jnp.int32)
    acts, grads, act_factors, grad_factors = acts[0], grads[0], act_factors[0], grad_factors[0]
    seq_dev = lengths.shape[0]
    tok_rows, width = acts.shape[0], act_factors.shape[1]
    rows = tok_rows // QUARTERS
    queries = width * loop_count // RANK

    other_grad = from_partner(grad_factors, "loop", 1)
    other_act = from_partner(act_factors, "loop", 1)

    own_shape = pltpu.VMEM((rows, 2 * width), jnp.float32)
    out_shape = pltpu.VMEM((rows + CODE_ROWS, 2 * width), jnp.int16)
    total_shape = pltpu.VMEM((QUARTERS, rows, width), jnp.float32)
    act_rows, grad_rows, mine, *mine_out = pl.pallas_call(
        own_kernel,
        name="own_columns",
        out_shape=(
            pltpu.VMEM(acts.shape, acts.dtype), pltpu.VMEM(grads.shape, grads.dtype),
            own_shape, out_shape, out_shape, out_shape,
        ),
        in_specs=[IN_SMEM, IN_HBM, IN_HBM, IN_HBM, IN_HBM],
        out_specs=(IN_VMEM,) * 6,
        scratch_shapes=[
            pltpu.VMEM(act_factors.shape, act_factors.dtype),
            pltpu.VMEM(grad_factors.shape, grad_factors.dtype),
            total_shape,
            pltpu.SemaphoreType.DMA((2, acts.shape[1] // CHUNK)),
            pltpu.SemaphoreType.DMA((2, grads.shape[1] // CHUNK)),
        ],
        compiler_params=pltpu.CompilerParams(vmem_limit_bytes=24 * MIB),
        cost_estimate=pl.CostEstimate(flops=2 * tok_rows * width * 9216, bytes_accessed=12 * MIB, transcendentals=0),
    )(place, acts, grads, act_factors, grad_factors)
    mine_in = [from_partner(mine_out[mask - 1], "layer", mask) for mask in range(1, QUARTERS)]

    vmem = lambda x: pltpu.with_memory_space_constraint(x, pltpu.VMEM)
    other, *other_out = pl.pallas_call(
        other_kernel,
        name="other_columns",
        out_shape=(own_shape, out_shape, out_shape, out_shape),
        in_specs=[IN_SMEM] + [IN_VMEM] * 4,
        out_specs=(IN_VMEM,) * 4,
        scratch_shapes=[total_shape],
        compiler_params=pltpu.CompilerParams(vmem_limit_bytes=24 * MIB),
        cost_estimate=pl.CostEstimate(flops=2 * tok_rows * width * 9216, bytes_accessed=0, transcendentals=0),
    )(place, vmem(act_rows), vmem(grad_rows), vmem(other_act), vmem(other_grad))
    other_in = [from_partner(other_out[mask - 1], "layer", mask) for mask in range(1, QUARTERS)]

    total = pl.pallas_call(
        score_kernel,
        name="scores",
        out_shape=pltpu.VMEM((seq_dev * loop_count, LANES), jnp.float32),
        in_specs=[IN_SMEM, IN_SMEM] + [IN_VMEM] * 8,
        out_specs=IN_VMEM,
    )(place, lengths, vmem(mine), *map(vmem, mine_in), vmem(other), *map(vmem, other_in))

    total = total + from_partner(total, "loop", 1)
    gathered = [from_partner(total, "layer", mask) for mask in range(1, QUARTERS)]
    total = total + gathered[0] + gathered[1] + gathered[2]
    mask = QUARTERS
    while mask < layer_count:
        total = total + from_partner(total, "layer", mask)
        mask *= 2
    return total[:, :queries]


def solution(mesh):
    in_specs = (
        P("layer", ("groups", "loop"), None),
        P("layer", ("groups", "loop"), None),
        P("layer", None, "loop"),
        P("layer", None, "loop"),
        P(("groups", "loop")),
    )
    out_specs = P("groups", None)
    return jax.shard_map(
        on_device, mesh=mesh, in_specs=in_specs, out_specs=out_specs, check_vma=False
    )
```

```python
import functools

import jax
import jax.numpy as jnp
from jax import lax
from jax.experimental import pallas as pl
from jax.experimental.pallas import tpu as pltpu
from jax.sharding import PartitionSpec as P

RANK = 32
QUARTERS = 4
LANES = 128
CODE_ROWS = 16
TOP = 32000.0
STEPS = 256.0
FLOOR = 2.0**-112
CHUNK = 1024
MIB = 2**20

IN_VMEM = pl.BlockSpec(memory_space=pltpu.VMEM)
IN_HBM = pl.BlockSpec(memory_space=pltpu.HBM)
IN_SMEM = pl.BlockSpec(memory_space=pltpu.SMEM)


def from_partner(value, axis, mask):
    pairs = [(source, source ^ mask) for source in range(lax.axis_size(axis))]
    return lax.ppermute(value, axis, pairs)


def dot(rows, factor):
    return jnp.dot(rows, factor, preferred_element_type=jnp.float32)


def encode(part):
    peak = jnp.max(jnp.abs(part), axis=0, keepdims=True)
    code = jnp.ceil(jnp.log2(jnp.maximum(peak, FLOOR)) * STEPS) + 1.0
    fixed = jnp.round(part * (TOP * jnp.exp2(code * (-1.0 / STEPS))))
    code = jnp.broadcast_to(code, (CODE_ROWS, part.shape[1]))
    return fixed.astype(jnp.int32).astype(jnp.int16), code.astype(jnp.int32).astype(jnp.int16)


def decode(message, rows):
    fixed = message[:rows, :].astype(jnp.int32).astype(jnp.float32)
    code = message[rows:, :].astype(jnp.int32).astype(jnp.float32)[:1]
    return fixed * (jnp.exp2(code * (1.0 / STEPS)) * (1.0 / TOP))


def share(total, quarter, own_ref, out_refs, first):
    rows = own_ref.shape[0]
    columns = slice(first, first + total.shape[2])
    own_ref[:, columns] = total[quarter]
    for mask in range(1, QUARTERS):
        fixed, code = encode(total[quarter ^ mask])
        out_refs[mask - 1][:rows, columns] = fixed
        out_refs[mask - 1][rows:, columns] = code


def own_kernel(place, acts, grads, act_factors, grad_factors,
               act_rows, grad_rows, own, out1, out2, out3,
               act_held, grad_held, total, act_sems, grad_sems):
    quarter = place[0]
    rows = own.shape[0]
    copies = []
    for source, rows_ref, factor, held, sems in (
        (acts, act_rows, act_factors, act_held, act_sems),
        (grads, grad_rows, grad_factors, grad_held, grad_sems),
    ):
        mine = []
        for step in range(source.shape[1] // CHUNK):
            depth = pl.ds(step * CHUNK, CHUNK)
            pair = (
                pltpu.make_async_copy(source.at[:, depth], rows_ref.at[:, depth], sems.at[0, step]),
                pltpu.make_async_copy(factor.at[depth, :], held.at[depth, :], sems.at[1, step]),
            )
            for copy in pair:
                copy.start()
            mine.append(pair)
        copies.append(mine)
    first = 0
    for mine, rows_ref, held in ((copies[0], act_rows, act_held), (copies[1], grad_rows, grad_held)):
        for step, pair in enumerate(mine):
            for copy in pair:
                copy.wait()
            depth = slice(step * CHUNK, (step + 1) * CHUNK)
            part = dot(rows_ref[:, depth], held[depth, :])
            for quarter_at in range(QUARTERS):
                block = part[quarter_at * rows:(quarter_at + 1) * rows]
                if step == 0:
                    total[quarter_at] = block
                else:
                    total[quarter_at] += block
        share(total, quarter, own, (out1, out2, out3), first)
        first += held.shape[1]


def other_kernel(place, act_rows, grad_rows, act_factors, grad_factors, own, out1, out2, out3, total):
    quarter = place[0]
    rows = own.shape[0]
    first = 0
    for rows_ref, factor in ((grad_rows, grad_factors), (act_rows, act_factors)):
        part = dot(rows_ref[...], factor[...])
        for quarter_at in range(QUARTERS):
            total[quarter_at] = part[quarter_at * rows:(quarter_at + 1) * rows]
        share(total, quarter, own, (out1, out2, out3), first)
        first += factor.shape[1]


def score_kernel(place, lengths, mine, mine1, mine2, mine3, other, other1, other2, other3, out):
    quarter, position = place[0], place[1]
    rows, width = mine.shape[0], mine.shape[1] // 2
    seq_part = lengths.shape[0] // QUARTERS
    pad_rows = rows // seq_part
    queries = width // RANK
    column = lax.broadcasted_iota(jnp.int32, (width, LANES), 0) // RANK
    lane = lax.broadcasted_iota(jnp.int32, (width, LANES), 1)
    offsets = lax.broadcasted_iota(jnp.int32, (pad_rows, width), 0)
    line = lax.broadcasted_iota(jnp.int32, out.shape, 0)
    result = jnp.zeros(out.shape, jnp.float32)
    units = (
        (mine, (mine1, mine2, mine3), position),
        (other, (other1, other2, other3), 1 - position),
    )
    for own, received, half in units:
        full = own[...]
        for message in received:
            full = full + decode(message[...], rows)
        pair = full[:, :width] * full[:, width:]
        pick = (lane == column + half * queries).astype(jnp.float32)
        for seq in range(seq_part):
            live = offsets < lengths[quarter * seq_part + seq]
            sums = jnp.sum(
                jnp.where(live, pair[seq * pad_rows:(seq + 1) * pad_rows], 0.0), axis=0, keepdims=True
            )
            sums = jnp.broadcast_to(sums, (8, width))
            scores = jnp.dot(
                sums, pick, precision=lax.Precision.HIGHEST, preferred_element_type=jnp.float32
            )[:1]
            at = (position * QUARTERS + quarter) * seq_part + seq
            result = result + jnp.where(line == at, scores, 0.0)
    out[...] = result


def on_device(acts, grads, act_factors, grad_factors, lengths):
    loop_count = lax.axis_size("loop")
    layer_count = lax.axis_size("layer")
    quarter = lax.axis_index("layer") % QUARTERS
    place = jnp.stack([quarter, lax.axis_index("loop")]).astype(jnp.int32)
    acts, grads, act_factors, grad_factors = acts[0], grads[0], act_factors[0], grad_factors[0]
    seq_dev = lengths.shape[0]
    tok_rows, width = acts.shape[0], act_factors.shape[1]
    rows = tok_rows // QUARTERS
    queries = width * loop_count // RANK

    other_grad = from_partner(grad_factors, "loop", 1)
    other_act = from_partner(act_factors, "loop", 1)

    own_shape = pltpu.VMEM((rows, 2 * width), jnp.float32)
    out_shape = pltpu.VMEM((rows + CODE_ROWS, 2 * width), jnp.int16)
    total_shape = pltpu.VMEM((QUARTERS, rows, width), jnp.float32)
    act_rows, grad_rows, mine, *mine_out = pl.pallas_call(
        own_kernel,
        name="own_columns",
        out_shape=(
            pltpu.VMEM(acts.shape, acts.dtype), pltpu.VMEM(grads.shape, grads.dtype),
            own_shape, out_shape, out_shape, out_shape,
        ),
        in_specs=[IN_SMEM, IN_HBM, IN_HBM, IN_HBM, IN_HBM],
        out_specs=(IN_VMEM,) * 6,
        scratch_shapes=[
            pltpu.VMEM(act_factors.shape, act_factors.dtype),
            pltpu.VMEM(grad_factors.shape, grad_factors.dtype),
            total_shape,
            pltpu.SemaphoreType.DMA((2, acts.shape[1] // CHUNK)),
            pltpu.SemaphoreType.DMA((2, grads.shape[1] // CHUNK)),
        ],
        compiler_params=pltpu.CompilerParams(vmem_limit_bytes=24 * MIB),
        cost_estimate=pl.CostEstimate(flops=2 * tok_rows * width * 9216, bytes_accessed=12 * MIB, transcendentals=0),
    )(place, *(pltpu.with_memory_space_constraint(x, pltpu.HBM) for x in (acts, grads, act_factors, grad_factors)))
    mine_in = [from_partner(mine_out[mask - 1], "layer", mask) for mask in range(1, QUARTERS)]

    vmem = lambda x: pltpu.with_memory_space_constraint(x, pltpu.VMEM)
    other, *other_out = pl.pallas_call(
        other_kernel,
        name="other_columns",
        out_shape=(own_shape, out_shape, out_shape, out_shape),
        in_specs=[IN_SMEM] + [IN_VMEM] * 4,
        out_specs=(IN_VMEM,) * 4,
        scratch_shapes=[total_shape],
        compiler_params=pltpu.CompilerParams(vmem_limit_bytes=24 * MIB),
        cost_estimate=pl.CostEstimate(flops=2 * tok_rows * width * 9216, bytes_accessed=0, transcendentals=0),
    )(place, vmem(act_rows), vmem(grad_rows), vmem(other_act), vmem(other_grad))
    other_in = [from_partner(other_out[mask - 1], "layer", mask) for mask in range(1, QUARTERS)]

    total = pl.pallas_call(
        score_kernel,
        name="scores",
        out_shape=pltpu.VMEM((seq_dev * loop_count, LANES), jnp.float32),
        in_specs=[IN_SMEM, IN_SMEM] + [IN_VMEM] * 8,
        out_specs=IN_VMEM,
    )(place, lengths, vmem(mine), *map(vmem, mine_in), vmem(other), *map(vmem, other_in))

    total = total + from_partner(total, "loop", 1)
    gathered = [from_partner(total, "layer", mask) for mask in range(1, QUARTERS)]
    total = total + gathered[0] + gathered[1] + gathered[2]
    mask = QUARTERS
    while mask < layer_count:
        total = total + from_partner(total, "layer", mask)
        mask *= 2
    return total[:, :queries]


def solution(mesh):
    in_specs = (
        P("layer", ("groups", "loop"), None),
        P("layer", ("groups", "loop"), None),
        P("layer", None, "loop"),
        P("layer", None, "loop"),
        P(("groups", "loop")),
    )
    out_specs = P("groups", None)
    return jax.shard_map(
        on_device, mesh=mesh, in_specs=in_specs, out_specs=out_specs, check_vma=False
    )
```

```python
import jax
import jax.numpy as jnp
from jax import lax
from jax.experimental import pallas as pl
from jax.experimental.pallas import tpu as pltpu
from jax.sharding import PartitionSpec as P

RANK = 32
QUARTERS = 4
LANES = 128
CODE_ROWS = 16
TOP = 32000.0
STEPS = 256.0
FLOOR = 2.0**-112
MIB = 2**20

IN_VMEM = pl.BlockSpec(memory_space=pltpu.VMEM)
IN_HBM = pl.BlockSpec(memory_space=pltpu.HBM)
IN_SMEM = pl.BlockSpec(memory_space=pltpu.SMEM)


def in_vmem(value):
    return pltpu.with_memory_space_constraint(value, pltpu.VMEM)


def in_hbm(value):
    return pltpu.with_memory_space_constraint(value, pltpu.HBM)


def from_partner(value, axis, mask):
    pairs = [(source, source ^ mask) for source in range(lax.axis_size(axis))]
    return lax.ppermute(value, axis, pairs)


def dot(rows, factor):
    return jnp.dot(rows, factor, preferred_element_type=jnp.float32)


def encode(part):
    peak = jnp.max(jnp.abs(part), axis=0, keepdims=True)
    code = jnp.ceil(jnp.log2(jnp.maximum(peak, FLOOR)) * STEPS) + 1.0
    fixed = jnp.round(part * (TOP * jnp.exp2(code * (-1.0 / STEPS))))
    code = jnp.broadcast_to(code, (CODE_ROWS, part.shape[1]))
    return fixed.astype(jnp.int32).astype(jnp.int16), code.astype(jnp.int32).astype(jnp.int16)


def decode(message, rows):
    fixed = message[:rows, :].astype(jnp.int32).astype(jnp.float32)
    code = message[rows:, :].astype(jnp.int32).astype(jnp.float32)[:1]
    return fixed * (jnp.exp2(code * (1.0 / STEPS)) * (1.0 / TOP))


def keep(part, total):
    rows = total.shape[1]
    for index in range(QUARTERS):
        total[index] = part[index * rows:(index + 1) * rows]


def share(total, quarter, own_ref, out_refs, first):
    rows = own_ref.shape[0]
    columns = slice(first, first + total.shape[2])
    own_ref[:, columns] = total[quarter]
    for mask in range(1, QUARTERS):
        fixed, code = encode(total[quarter ^ mask])
        out_refs[mask - 1][:rows, columns] = fixed
        out_refs[mask - 1][rows:, columns] = code


def act_own_kernel(acts, factor, total, rows_held, factor_held, sems):
    copies = (
        pltpu.make_async_copy(factor, factor_held, sems.at[0]),
        pltpu.make_async_copy(acts, rows_held, sems.at[1]),
    )
    for copy in copies:
        copy.start()
    for copy in copies:
        copy.wait()
    keep(dot(rows_held[...], factor_held[...]), total)


def grad_own_kernel(grads, factor, after, total):
    keep(dot(grads[...], factor[...]), total)


def other_kernel(*refs):
    *held, other_factor, mine, own, out1, out2, out3, total = refs
    quarter = lax.axis_index("layer") % QUARTERS
    outs = (out1, out2, out3)
    share(mine, quarter, own, outs, 0)
    first, part = 0, 0.0
    for rows_held in held:
        depth = rows_held.shape[1]
        part = part + dot(rows_held[...], other_factor[first:first + depth, :])
        first += depth
    keep(part, total)
    share(total, quarter, own, outs, total.shape[2])


def sum_kernel(own, in1, in2, in3, out):
    rows = own.shape[0]
    full = own[...]
    for message in (in1, in2, in3):
        full = full + decode(message[...], rows)
    out[...] = full


def score_kernel(lengths, acts, own, in1, in2, in3, out):
    quarter, position = lax.axis_index("layer") % QUARTERS, lax.axis_index("loop")
    rows, width = own.shape
    seq_part = lengths.shape[0] // QUARTERS
    pad_rows = rows // seq_part
    half = width // 2
    queries = half // RANK
    column = lax.broadcasted_iota(jnp.int32, (width, LANES), 0)
    lane = lax.broadcasted_iota(jnp.int32, (width, LANES), 1)
    holder = jnp.where(column < half, position, 1 - position)
    pick = (lane == (column % half) // RANK + holder * queries).astype(jnp.float32)
    offsets = lax.broadcasted_iota(jnp.int32, (pad_rows, width), 0)
    line = lax.broadcasted_iota(jnp.int32, out.shape, 0)
    full = own[...]
    for message in (in1, in2, in3):
        full = full + decode(message[...], rows)
    pair = acts[...] * full
    result = jnp.zeros(out.shape, jnp.float32)
    for seq in range(seq_part):
        live = offsets < lengths[quarter * seq_part + seq]
        sums = jnp.sum(
            jnp.where(live, pair[seq * pad_rows:(seq + 1) * pad_rows], 0.0), axis=0, keepdims=True
        )
        scores = jnp.dot(
            jnp.broadcast_to(sums, (8, width)), pick,
            precision=lax.Precision.HIGHEST, preferred_element_type=jnp.float32,
        )[:1]
        at = (position * QUARTERS + quarter) * seq_part + seq
        result = result + jnp.where(line == at, scores, 0.0)
    out[...] = result


def on_device(acts, grads, act_factors, grad_factors, lengths):
    loop_count = lax.axis_size("loop")
    layer_count = lax.axis_size("layer")
    acts, grads, act_factors, grad_factors = acts[0], grads[0], act_factors[0], grad_factors[0]
    seq_dev = lengths.shape[0]
    tok_rows, width = acts.shape[0], act_factors.shape[1]
    rows = tok_rows // QUARTERS
    queries = width * loop_count // RANK

    own_shape = pltpu.VMEM((rows, 2 * width), jnp.float32)
    out_shape = pltpu.VMEM((rows + CODE_ROWS, 2 * width), jnp.int16)
    total_shape = pltpu.VMEM((QUARTERS, rows, width), jnp.float32)

    def cost(depth, mib):
        return pl.CostEstimate(
            flops=2 * tok_rows * width * depth, bytes_accessed=mib * MIB, transcendentals=0
        )

    def limit(mib):
        return pltpu.CompilerParams(vmem_limit_bytes=mib * MIB)

    def other_columns(name, held, other_factor, mine, mib):
        own, *outs = pl.pallas_call(
            other_kernel,
            name=name,
            out_shape=(own_shape, out_shape, out_shape, out_shape),
            in_specs=[IN_VMEM] * (len(held) + 2),
            out_specs=(IN_VMEM,) * 4,
            scratch_shapes=[total_shape],
            compiler_params=limit(8),
            cost_estimate=cost(other_factor.shape[0], mib),
        )(*map(in_vmem, held), in_vmem(other_factor), in_vmem(mine))
        return own, [from_partner(outs[mask - 1], "layer", mask) for mask in range(1, QUARTERS)]

    other_act = from_partner(act_factors, "loop", 1)
    act_mine, act_rows = pl.pallas_call(
        act_own_kernel,
        name="act_own_columns",
        out_shape=(total_shape, pltpu.VMEM(acts.shape, acts.dtype)),
        in_specs=[IN_HBM] * 2,
        out_specs=(IN_VMEM,) * 2,
        scratch_shapes=[
            pltpu.VMEM(act_factors.shape, act_factors.dtype),
            pltpu.SemaphoreType.DMA((2,)),
        ],
        compiler_params=limit(8),
        cost_estimate=cost(acts.shape[1], 20),
    )(in_hbm(acts), in_hbm(act_factors))
    later_factors, other_act, act_mine = lax.optimization_barrier((grad_factors, other_act, act_mine))
    other_grad = from_partner(later_factors, "loop", 1)
    act_own, act_in = other_columns("act_other_columns", [act_rows], other_act, act_mine, 20)

    grad_mine = pl.pallas_call(
        grad_own_kernel,
        name="grad_own_columns",
        out_shape=total_shape,
        in_specs=[IN_VMEM] * 3,
        out_specs=IN_VMEM,
        compiler_params=limit(8),
        cost_estimate=cost(grads.shape[1], 10),
    )(in_vmem(grads), in_vmem(grad_factors), in_vmem(act_own))
    grad_own, grad_in = other_columns("grad_other_columns", [grads], other_grad, grad_mine, 10)

    act_full = pl.pallas_call(
        sum_kernel,
        name="act_sum",
        out_shape=own_shape,
        in_specs=[IN_VMEM] * 4,
        out_specs=IN_VMEM,
        compiler_params=limit(8),
    )(in_vmem(act_own), *map(in_vmem, act_in))
    total = pl.pallas_call(
        score_kernel,
        name="scores",
        out_shape=pltpu.VMEM((seq_dev * loop_count, LANES), jnp.float32),
        in_specs=[IN_SMEM] + [IN_VMEM] * 5,
        out_specs=IN_VMEM,
        compiler_params=limit(8),
    )(lengths, in_vmem(act_full), in_vmem(grad_own), *map(in_vmem, grad_in))

    total = total + from_partner(total, "loop", 1)
    gathered = [from_partner(total, "layer", mask) for mask in range(1, QUARTERS)]
    total = total + gathered[0] + gathered[1] + gathered[2]
    mask = QUARTERS
    while mask < layer_count:
        total = total + from_partner(total, "layer", mask)
        mask *= 2
    return total[:, :queries]


def solution(mesh):
    in_specs = (
        P("layer", ("groups", "loop"), None),
        P("layer", ("groups", "loop"), None),
        P("layer", None, "loop"),
        P("layer", None, "loop"),
        P(("groups", "loop")),
    )
    out_specs = P("groups", None)
    return jax.shard_map(
        on_device, mesh=mesh, in_specs=in_specs, out_specs=out_specs, check_vma=False
    )
```

```python
import jax
import jax.numpy as jnp
from jax import lax
from jax.experimental import pallas as pl
from jax.experimental.pallas import tpu as pltpu
from jax.sharding import PartitionSpec as P

RANK = 32
QUARTERS = 4
LANES = 128
CODE_ROWS = 16
TOP = 32000.0
STEPS = 256.0
FLOOR = 2.0**-112
MIB = 2**20
ACT_OWN_MIB = 50

IN_VMEM = pl.BlockSpec(memory_space=pltpu.VMEM)
IN_HBM = pl.BlockSpec(memory_space=pltpu.HBM)
IN_SMEM = pl.BlockSpec(memory_space=pltpu.SMEM)


def in_vmem(value):
    return pltpu.with_memory_space_constraint(value, pltpu.VMEM)


def in_hbm(value):
    return pltpu.with_memory_space_constraint(value, pltpu.HBM)


def from_partner(value, axis, mask):
    pairs = [(source, source ^ mask) for source in range(lax.axis_size(axis))]
    return lax.ppermute(value, axis, pairs)


def dot(rows, factor):
    return jnp.dot(rows, factor, preferred_element_type=jnp.float32)


def encode(part):
    peak = jnp.max(jnp.abs(part), axis=0, keepdims=True)
    code = jnp.ceil(jnp.log2(jnp.maximum(peak, FLOOR)) * STEPS) + 1.0
    fixed = jnp.round(part * (TOP * jnp.exp2(code * (-1.0 / STEPS))))
    code = jnp.broadcast_to(code, (CODE_ROWS, part.shape[1]))
    return fixed.astype(jnp.int32).astype(jnp.int16), code.astype(jnp.int32).astype(jnp.int16)


def decode(message, rows):
    fixed = message[:rows, :].astype(jnp.int32).astype(jnp.float32)
    code = message[rows:, :].astype(jnp.int32).astype(jnp.float32)[:1]
    return fixed * (jnp.exp2(code * (1.0 / STEPS)) * (1.0 / TOP))


def keep(part, total):
    rows = total.shape[1]
    for index in range(QUARTERS):
        total[index] = part[index * rows:(index + 1) * rows]


def share(total, quarter, own_ref, out_refs, first):
    rows = own_ref.shape[0]
    columns = slice(first, first + total.shape[2])
    own_ref[:, columns] = total[quarter]
    for mask in range(1, QUARTERS):
        fixed, code = encode(total[quarter ^ mask])
        out_refs[mask - 1][:rows, columns] = fixed
        out_refs[mask - 1][rows:, columns] = code


def act_own_kernel(acts, factor, grad_factor, total, rows_held, grad_factor_held, factor_held, sems):
    copies = (
        pltpu.make_async_copy(factor, factor_held, sems.at[0]),
        pltpu.make_async_copy(acts, rows_held, sems.at[1]),
        pltpu.make_async_copy(grad_factor, grad_factor_held, sems.at[2]),
    )
    for copy in copies:
        copy.start()
    copies[0].wait()
    copies[1].wait()
    keep(dot(rows_held[...], factor_held[...]), total)
    copies[2].wait()


def grad_own_kernel(grads, factor, total):
    keep(dot(grads[...], factor[...]), total)


def act_other_kernel(act_held, other_factor, act_total, grad_total, own, out1, out2, out3, total):
    quarter = lax.axis_index("layer") % QUARTERS
    outs = (out1, out2, out3)
    width = total.shape[2]
    keep(dot(act_held[...], other_factor[...]), total)
    for index, part in enumerate((act_total, grad_total, total)):
        share(part, quarter, own, outs, index * width)


def grad_other_kernel(grads, other_factor, own, out1, out2, out3, total):
    quarter = lax.axis_index("layer") % QUARTERS
    keep(dot(grads[...], other_factor[...]), total)
    share(total, quarter, own, (out1, out2, out3), 0)


def received(own, messages):
    full = own[...]
    for message in messages:
        full = full + decode(message[...], own.shape[0])
    return full


def score(pair, lengths, holder, out):
    quarter, position = lax.axis_index("layer") % QUARTERS, lax.axis_index("loop")
    rows, width = pair.shape
    seq_part = lengths.shape[0] // QUARTERS
    pad_rows = rows // seq_part
    column = lax.broadcasted_iota(jnp.int32, (width, LANES), 0)
    lane = lax.broadcasted_iota(jnp.int32, (width, LANES), 1)
    pick = (lane == column // RANK + holder * (width // RANK)).astype(jnp.float32)
    offsets = lax.broadcasted_iota(jnp.int32, (pad_rows, width), 0)
    line = lax.broadcasted_iota(jnp.int32, out.shape, 0)
    result = jnp.zeros(out.shape, jnp.float32)
    for seq in range(seq_part):
        live = offsets < lengths[quarter * seq_part + seq]
        sums = jnp.sum(
            jnp.where(live, pair[seq * pad_rows:(seq + 1) * pad_rows], 0.0), axis=0, keepdims=True
        )
        scores = jnp.dot(
            jnp.broadcast_to(sums, (8, width)), pick,
            precision=lax.Precision.HIGHEST, preferred_element_type=jnp.float32,
        )[:1]
        at = (position * QUARTERS + quarter) * seq_part + seq
        result = result + jnp.where(line == at, scores, 0.0)
    return result


def own_score_kernel(lengths, own, in1, in2, in3, out, act_other):
    width = act_other.shape[1]
    full = received(own, (in1, in2, in3))
    act_other[...] = full[:, 2 * width:]
    out[...] = score(full[:, :width] * full[:, width:2 * width], lengths, lax.axis_index("loop"), out)


def other_score_kernel(lengths, act_other, before, own, in1, in2, in3, out):
    pair = act_other[...] * received(own, (in1, in2, in3))
    out[...] = before[...] + score(pair, lengths, 1 - lax.axis_index("loop"), out)


def on_device(acts, grads, act_factors, grad_factors, lengths):
    loop_count = lax.axis_size("loop")
    layer_count = lax.axis_size("layer")
    acts, grads, act_factors, grad_factors = acts[0], grads[0], act_factors[0], grad_factors[0]
    seq_dev = lengths.shape[0]
    tok_rows, width = acts.shape[0], act_factors.shape[1]
    rows = tok_rows // QUARTERS
    queries = width * loop_count // RANK

    depth = grads.shape[1]

    def kernel(body, name, outs, specs, scratch, mib, work):
        return pl.pallas_call(
            body,
            name=name,
            out_shape=tuple(outs),
            in_specs=specs,
            out_specs=(IN_VMEM,) * len(outs),
            scratch_shapes=scratch,
            compiler_params=pltpu.CompilerParams(vmem_limit_bytes=mib * MIB),
            cost_estimate=pl.CostEstimate(
                flops=2 * tok_rows * width * work, bytes_accessed=mib * MIB, transcendentals=0
            ),
        )

    def own_shape(parts):
        return pltpu.VMEM((rows, parts * width), jnp.float32)

    def out_shapes(parts):
        return [pltpu.VMEM((rows + CODE_ROWS, parts * width), jnp.int16)] * (QUARTERS - 1)

    def to_quarters(outs):
        return [in_vmem(from_partner(outs[mask - 1], "layer", mask)) for mask in range(1, QUARTERS)]

    total_shape = pltpu.VMEM((QUARTERS, rows, width), jnp.float32)
    score_shape = pltpu.VMEM((seq_dev * loop_count, LANES), jnp.float32)

    other_act = from_partner(act_factors, "loop", 1)
    act_total, act_held, factor_held = kernel(
        act_own_kernel, "act_own_columns",
        (total_shape, pltpu.VMEM(acts.shape, acts.dtype), pltpu.VMEM(grad_factors.shape, grad_factors.dtype)),
        [IN_HBM] * 3,
        [pltpu.VMEM(act_factors.shape, act_factors.dtype), pltpu.SemaphoreType.DMA((3,))],
        ACT_OWN_MIB, acts.shape[1],
    )(in_hbm(acts), in_hbm(act_factors), in_hbm(grad_factors))
    later_factors, other_act, act_total = lax.optimization_barrier((grad_factors, other_act, act_total))
    other_grad = from_partner(later_factors, "loop", 1)
    (grad_total,) = kernel(
        grad_own_kernel, "grad_own_columns", (total_shape,), [IN_VMEM] * 2, [], 8, depth,
    )(in_vmem(grads), in_vmem(factor_held))
    own, *outs = kernel(
        act_other_kernel, "act_other_columns", (own_shape(3), *out_shapes(3)), [IN_VMEM] * 4, [total_shape],
        8, acts.shape[1],
    )(in_vmem(act_held), in_vmem(other_act), in_vmem(act_total), in_vmem(grad_total))
    own_in = to_quarters(outs)
    other, *outs = kernel(
        grad_other_kernel, "grad_other_columns", (own_shape(1), *out_shapes(1)), [IN_VMEM] * 2, [total_shape],
        8, depth,
    )(in_vmem(grads), in_vmem(other_grad))
    other_in = to_quarters(outs)
    before, act_other = kernel(
        own_score_kernel, "own_scores", (score_shape, own_shape(1)), [IN_SMEM] + [IN_VMEM] * 4, [], 8, 0,
    )(lengths, in_vmem(own), *own_in)
    (total,) = kernel(
        other_score_kernel, "other_scores", (score_shape,), [IN_SMEM] + [IN_VMEM] * 6, [], 8, 0,
    )(lengths, in_vmem(act_other), in_vmem(before), in_vmem(other), *other_in)

    total = total + from_partner(total, "loop", 1)
    gathered = [from_partner(total, "layer", mask) for mask in range(1, QUARTERS)]
    total = total + gathered[0] + gathered[1] + gathered[2]
    mask = QUARTERS
    while mask < layer_count:
        total = total + from_partner(total, "layer", mask)
        mask *= 2
    return total[:, :queries]


def solution(mesh):
    in_specs = (
        P("layer", ("groups", "loop"), None),
        P("layer", ("groups", "loop"), None),
        P("layer", None, "loop"),
        P("layer", None, "loop"),
        P(("groups", "loop")),
    )
    out_specs = P("groups", None)
    return jax.shard_map(
        on_device, mesh=mesh, in_specs=in_specs, out_specs=out_specs, check_vma=False
    )
```

```python
import jax
import jax.numpy as jnp
from jax import lax
from jax.experimental import pallas as pl
from jax.experimental.pallas import tpu as pltpu
from jax.sharding import PartitionSpec as P

RANK = 32
QUARTERS = 4
LANES = 128
CODE_ROWS = 16
TOP = 32000.0
STEPS = 256.0
FLOOR = 2.0**-112
MIB = 2**20
ACT_OWN_MIB = 50

IN_VMEM = pl.BlockSpec(memory_space=pltpu.VMEM)
IN_HBM = pl.BlockSpec(memory_space=pltpu.HBM)
IN_SMEM = pl.BlockSpec(memory_space=pltpu.SMEM)


def in_vmem(value):
    return pltpu.with_memory_space_constraint(value, pltpu.VMEM)


def in_hbm(value):
    return pltpu.with_memory_space_constraint(value, pltpu.HBM)


def from_partner(value, axis, mask):
    pairs = [(source, source ^ mask) for source in range(lax.axis_size(axis))]
    return lax.ppermute(value, axis, pairs)


def dot(rows, factor):
    return jnp.dot(rows, factor, preferred_element_type=jnp.float32)


def encode(part):
    peak = jnp.max(jnp.abs(part), axis=0, keepdims=True)
    code = jnp.ceil(jnp.log2(jnp.maximum(peak, FLOOR)) * STEPS) + 1.0
    fixed = jnp.round(part * (TOP * jnp.exp2(code * (-1.0 / STEPS))))
    code = jnp.broadcast_to(code, (CODE_ROWS, part.shape[1]))
    return fixed.astype(jnp.int32).astype(jnp.int16), code.astype(jnp.int32).astype(jnp.int16)


def decode(message, rows):
    fixed = message[:rows, :].astype(jnp.int32).astype(jnp.float32)
    code = message[rows:, :].astype(jnp.int32).astype(jnp.float32)[:1]
    return fixed * (jnp.exp2(code * (1.0 / STEPS)) * (1.0 / TOP))


def keep(part, total):
    rows = total.shape[1]
    for index in range(QUARTERS):
        total[index] = part[index * rows:(index + 1) * rows]


def share(total, quarter, own_ref, out_refs, first):
    rows = own_ref.shape[0]
    columns = slice(first, first + total.shape[2])
    own_ref[:, columns] = total[quarter]
    for mask in range(1, QUARTERS):
        fixed, code = encode(total[quarter ^ mask])
        out_refs[mask - 1][:rows, columns] = fixed
        out_refs[mask - 1][rows:, columns] = code


def act_own_kernel(acts, factor, grad_factor, total, rows_held, grad_factor_held, factor_held, sems):
    copies = (
        pltpu.make_async_copy(factor, factor_held, sems.at[0]),
        pltpu.make_async_copy(acts, rows_held, sems.at[1]),
        pltpu.make_async_copy(grad_factor, grad_factor_held, sems.at[2]),
    )
    for copy in copies:
        copy.start()
    copies[0].wait()
    copies[1].wait()
    keep(dot(rows_held[...], factor_held[...]), total)
    copies[2].wait()


def grad_own_kernel(grads, factor, total):
    keep(dot(grads[...], factor[...]), total)


def act_other_kernel(act_held, other_factor, act_total, grad_total, own, out1, out2, out3, total):
    quarter = lax.axis_index("layer") % QUARTERS
    outs = (out1, out2, out3)
    width = total.shape[2]
    keep(dot(act_held[...], other_factor[...]), total)
    for index, part in enumerate((act_total, grad_total, total)):
        share(part, quarter, own, outs, index * width)


def grad_other_kernel(grads, other_factor, own, out1, out2, out3, total):
    quarter = lax.axis_index("layer") % QUARTERS
    keep(dot(grads[...], other_factor[...]), total)
    share(total, quarter, own, (out1, out2, out3), 0)


def received(own, messages):
    full = own[...]
    for message in messages:
        full = full + decode(message[...], own.shape[0])
    return full


def score(pair, lengths, holder, out):
    quarter, position = lax.axis_index("layer") % QUARTERS, lax.axis_index("loop")
    rows, width = pair.shape
    seq_part = lengths.shape[0] // QUARTERS
    pad_rows = rows // seq_part
    column = lax.broadcasted_iota(jnp.int32, (width, LANES), 0)
    lane = lax.broadcasted_iota(jnp.int32, (width, LANES), 1)
    pick = (lane == column // RANK + holder * (width // RANK)).astype(jnp.float32)
    offsets = lax.broadcasted_iota(jnp.int32, (pad_rows, width), 0)
    line = lax.broadcasted_iota(jnp.int32, out.shape, 0)
    result = jnp.zeros(out.shape, jnp.float32)
    for seq in range(seq_part):
        live = offsets < lengths[quarter * seq_part + seq]
        sums = jnp.sum(
            jnp.where(live, pair[seq * pad_rows:(seq + 1) * pad_rows], 0.0), axis=0, keepdims=True
        )
        scores = jnp.dot(
            jnp.broadcast_to(sums, (8, width)), pick,
            precision=lax.Precision.HIGHEST, preferred_element_type=jnp.float32,
        )[:1]
        at = (position * QUARTERS + quarter) * seq_part + seq
        result = result + jnp.where(line == at, scores, 0.0)
    return result


def own_score_kernel(lengths, own, in1, in2, in3, out, act_other):
    width = act_other.shape[1]
    full = received(own, (in1, in2, in3))
    act_other[...] = full[:, 2 * width:]
    out[...] = score(full[:, :width] * full[:, width:2 * width], lengths, lax.axis_index("loop"), out)


def other_score_kernel(lengths, act_other, before, own, in1, in2, in3, out):
    pair = act_other[...] * received(own, (in1, in2, in3))
    out[...] = before[...] + score(pair, lengths, 1 - lax.axis_index("loop"), out)


def on_device(acts, grads, act_factors, grad_factors, lengths):
    loop_count = lax.axis_size("loop")
    layer_count = lax.axis_size("layer")
    acts, grads, act_factors, grad_factors = acts[0], grads[0], act_factors[0], grad_factors[0]
    seq_dev = lengths.shape[0]
    tok_rows, width = acts.shape[0], act_factors.shape[1]
    rows = tok_rows // QUARTERS
    queries = width * loop_count // RANK

    depth = grads.shape[1]

    def kernel(body, name, outs, specs, scratch, mib, work):
        return pl.pallas_call(
            body,
            name=name,
            out_shape=tuple(outs),
            in_specs=specs,
            out_specs=(IN_VMEM,) * len(outs),
            scratch_shapes=scratch,
            compiler_params=pltpu.CompilerParams(vmem_limit_bytes=mib * MIB),
            cost_estimate=pl.CostEstimate(
                flops=2 * tok_rows * width * work, bytes_accessed=mib * MIB, transcendentals=0
            ),
        )

    def own_shape(parts):
        return pltpu.VMEM((rows, parts * width), jnp.float32)

    def out_shapes(parts):
        return [pltpu.VMEM((rows + CODE_ROWS, parts * width), jnp.int16)] * (QUARTERS - 1)

    def to_quarters(outs):
        return [in_vmem(from_partner(outs[mask - 1], "layer", mask)) for mask in range(1, QUARTERS)]

    total_shape = pltpu.VMEM((QUARTERS, rows, width), jnp.float32)
    score_shape = pltpu.VMEM((seq_dev * loop_count, LANES), jnp.float32)

    other_act = from_partner(act_factors, "loop", 1)
    act_total, act_held, factor_held = kernel(
        act_own_kernel, "act_own_columns",
        (total_shape, pltpu.VMEM(acts.shape, acts.dtype), pltpu.VMEM(grad_factors.shape, grad_factors.dtype)),
        [IN_HBM] * 3,
        [pltpu.VMEM(act_factors.shape, act_factors.dtype), pltpu.SemaphoreType.DMA((3,))],
        ACT_OWN_MIB, acts.shape[1],
    )(in_hbm(acts), in_hbm(act_factors), in_hbm(grad_factors))
    later_factors, other_act, act_total = lax.optimization_barrier((grad_factors, other_act, act_total))
    other_grad = from_partner(later_factors, "loop", 1)
    (grad_total,) = kernel(
        grad_own_kernel, "grad_own_columns", (total_shape,), [IN_VMEM] * 2, [], 8, depth,
    )(in_vmem(grads), in_vmem(factor_held))
    own, *outs = kernel(
        act_other_kernel, "act_other_columns", (own_shape(3), *out_shapes(3)), [IN_VMEM] * 4, [total_shape],
        8, acts.shape[1],
    )(in_vmem(act_held), in_vmem(other_act), in_vmem(act_total), in_vmem(grad_total))
    own_in = to_quarters(outs)
    other, *outs = kernel(
        grad_other_kernel, "grad_other_columns", (own_shape(1), *out_shapes(1)), [IN_VMEM] * 2, [total_shape],
        8, depth,
    )(in_vmem(grads), in_vmem(other_grad))
    other_in = to_quarters(outs)
    before, act_other = kernel(
        own_score_kernel, "own_scores", (score_shape, own_shape(1)), [IN_SMEM] + [IN_VMEM] * 4, [], 8, 0,
    )(lengths, in_vmem(own), *own_in)
    (total,) = kernel(
        other_score_kernel, "other_scores", (score_shape,), [IN_SMEM] + [IN_VMEM] * 6, [], 8, 0,
    )(lengths, in_vmem(act_other), in_vmem(before), in_vmem(other), *other_in)

    total = total + from_partner(total, "loop", 1)
    both = ("layer", "loop")
    gathered = [from_partner(total, both, (mask + 1) * loop_count - 1) for mask in range(1, QUARTERS)]
    total = total + gathered[0] + gathered[1] + gathered[2]
    mask = QUARTERS
    while mask < layer_count:
        total = total + from_partner(total, both, (mask + 1) * loop_count - 1)
        mask *= 2
    return total[:, :queries]


def solution(mesh):
    in_specs = (
        P("layer", ("groups", "loop"), None),
        P("layer", ("groups", "loop"), None),
        P("layer", None, "loop"),
        P("layer", None, "loop"),
        P(("groups", "loop")),
    )
    out_specs = P("groups", None)
    return jax.shard_map(
        on_device, mesh=mesh, in_specs=in_specs, out_specs=out_specs, check_vma=False
    )
```

```python
import functools

import jax
import jax.numpy as jnp
from jax import lax
from jax.experimental import pallas as pl
from jax.experimental.pallas import tpu as pltpu
from jax.sharding import PartitionSpec as P

RANK = 32
QUARTERS = 4
LANES = 128
CODE_ROWS = 16
TOP = 32000.0
STEPS = 256.0
FLOOR = 2.0**-112
MIB = 2**20
ACT_OWN_MIB = 50

IN_VMEM = pl.BlockSpec(memory_space=pltpu.VMEM)
IN_HBM = pl.BlockSpec(memory_space=pltpu.HBM)
IN_SMEM = pl.BlockSpec(memory_space=pltpu.SMEM)


def in_vmem(value):
    return pltpu.with_memory_space_constraint(value, pltpu.VMEM)


def in_hbm(value):
    return pltpu.with_memory_space_constraint(value, pltpu.HBM)


def from_partner(value, axis, mask):
    pairs = [(source, source ^ mask) for source in range(lax.axis_size(axis))]
    return lax.ppermute(value, axis, pairs)


def dot(rows, factor):
    return jnp.dot(rows, factor, preferred_element_type=jnp.float32)


def encode(part):
    peak = jnp.max(jnp.abs(part), axis=0, keepdims=True)
    code = jnp.ceil(jnp.log2(jnp.maximum(peak, FLOOR)) * STEPS) + 1.0
    fixed = jnp.round(part * (TOP * jnp.exp2(code * (-1.0 / STEPS))))
    code = jnp.broadcast_to(code, (CODE_ROWS, part.shape[1]))
    return fixed.astype(jnp.int32).astype(jnp.int16), code.astype(jnp.int32).astype(jnp.int16)


def decode(message, rows):
    fixed = message[:rows, :].astype(jnp.int32).astype(jnp.float32)
    code = message[rows:, :].astype(jnp.int32).astype(jnp.float32)[:1]
    return fixed * (jnp.exp2(code * (1.0 / STEPS)) * (1.0 / TOP))


def keep(part, total):
    rows = total.shape[1]
    for index in range(QUARTERS):
        total[index] = part[index * rows:(index + 1) * rows]


def share(total, quarter, own_ref, out_refs, first):
    rows = own_ref.shape[0]
    columns = slice(first, first + total.shape[2])
    own_ref[:, columns] = total[quarter]
    for mask in range(1, QUARTERS):
        fixed, code = encode(total[quarter ^ mask])
        out_refs[mask - 1][:rows, columns] = fixed
        out_refs[mask - 1][rows:, columns] = code


def act_own_kernel(acts, factor, grad_factor, total, rows_held, grad_factor_held, factor_held, sems):
    copies = (
        pltpu.make_async_copy(factor, factor_held, sems.at[0]),
        pltpu.make_async_copy(acts, rows_held, sems.at[1]),
        pltpu.make_async_copy(grad_factor, grad_factor_held, sems.at[2]),
    )
    for copy in copies:
        copy.start()
    copies[0].wait()
    copies[1].wait()
    keep(dot(rows_held[...], factor_held[...]), total)
    copies[2].wait()


def grad_own_kernel(grads, factor, total):
    keep(dot(grads[...], factor[...]), total)


def act_other_kernel(act_held, other_factor, act_total, grad_total, own, out1, out2, out3, total):
    quarter = lax.axis_index("layer") % QUARTERS
    outs = (out1, out2, out3)
    width = total.shape[2]
    keep(dot(act_held[...], other_factor[...]), total)
    for index, part in enumerate((act_total, grad_total, total)):
        share(part, quarter, own, outs, index * width)


def grad_other_kernel(grads, other_factor, own, out1, out2, out3, total):
    quarter = lax.axis_index("layer") % QUARTERS
    keep(dot(grads[...], other_factor[...]), total)
    share(total, quarter, own, (out1, out2, out3), 0)


def received(own, messages):
    full = own[...]
    for message in messages:
        full = full + decode(message[...], own.shape[0])
    return full


def score(pair, seq_part, holder, out):
    quarter, position = lax.axis_index("layer") % QUARTERS, lax.axis_index("loop")
    rows, width = pair.shape
    pad_rows = rows // seq_part
    column = lax.broadcasted_iota(jnp.int32, (width, LANES), 0)
    lane = lax.broadcasted_iota(jnp.int32, (width, LANES), 1)
    pick = (lane == column // RANK + holder * (width // RANK)).astype(jnp.float32).astype(jnp.bfloat16)
    line = lax.broadcasted_iota(jnp.int32, out.shape, 0)
    result = jnp.zeros(out.shape, jnp.float32)
    for seq in range(seq_part):
        sums = jnp.sum(pair[seq * pad_rows:(seq + 1) * pad_rows], axis=0, keepdims=True)
        high = sums.astype(jnp.bfloat16).astype(jnp.float32)
        middle = (sums - high).astype(jnp.bfloat16).astype(jnp.float32)
        low = sums - high - middle
        term = lax.broadcasted_iota(jnp.int32, (8, width), 0)
        terms = jnp.where(term == 0, high, jnp.where(term == 1, middle, jnp.where(term == 2, low, 0.0)))
        scores = jnp.sum(dot(terms.astype(jnp.bfloat16), pick), axis=0, keepdims=True)
        at = (position * QUARTERS + quarter) * seq_part + seq
        result = result + jnp.where(line == at, scores, 0.0)
    return result


def own_score_kernel(lengths, own, in1, in2, in3, out, act_other):
    rows, width = act_other.shape
    seq_part = lengths.shape[0] // QUARTERS
    pad_rows = rows // seq_part
    quarter = lax.axis_index("layer") % QUARTERS
    full = received(own, (in1, in2, in3))
    offset = lax.broadcasted_iota(jnp.int32, (rows, width), 0)
    live = jnp.zeros((rows, width), jnp.bool_)
    for seq in range(seq_part):
        first = seq * pad_rows
        live = live | ((offset >= first) & (offset < first + lengths[quarter * seq_part + seq]))
    act_other[...] = jnp.where(live, full[:, 2 * width:], 0.0)
    pair = jnp.where(live, full[:, :width], 0.0) * full[:, width:2 * width]
    out[...] = score(pair, seq_part, lax.axis_index("loop"), out)


def other_score_kernel(seq_part, act_other, before, own, in1, in2, in3, out):
    pair = act_other[...] * received(own, (in1, in2, in3))
    out[...] = before[...] + score(pair, seq_part, 1 - lax.axis_index("loop"), out)


def on_device(acts, grads, act_factors, grad_factors, lengths):
    both = ("layer", "loop")
    loop_count = lax.axis_size("loop")
    layer_count = lax.axis_size("layer")
    acts, grads, act_factors, grad_factors = acts[0], grads[0], act_factors[0], grad_factors[0]
    seq_dev = lengths.shape[0]
    tok_rows, width = acts.shape[0], act_factors.shape[1]
    rows = tok_rows // QUARTERS
    queries = width * loop_count // RANK

    depth = grads.shape[1]

    def kernel(body, name, outs, specs, scratch, mib, work):
        return pl.pallas_call(
            body,
            name=name,
            out_shape=tuple(outs),
            in_specs=specs,
            out_specs=(IN_VMEM,) * len(outs),
            scratch_shapes=scratch,
            compiler_params=pltpu.CompilerParams(vmem_limit_bytes=mib * MIB),
            cost_estimate=pl.CostEstimate(
                flops=2 * tok_rows * width * work, bytes_accessed=mib * MIB, transcendentals=0
            ),
        )

    def own_shape(parts):
        return pltpu.VMEM((rows, parts * width), jnp.float32)

    def out_shapes(parts):
        return [pltpu.VMEM((rows + CODE_ROWS, parts * width), jnp.int16)] * (QUARTERS - 1)

    def to_quarters(outs):
        return [in_vmem(from_partner(outs[mask - 1], "layer", mask)) for mask in range(1, QUARTERS)]

    total_shape = pltpu.VMEM((QUARTERS, rows, width), jnp.float32)
    score_shape = pltpu.VMEM((seq_dev * loop_count, LANES), jnp.float32)

    other_act = from_partner(act_factors, "loop", 1)
    act_total, act_held, factor_held = kernel(
        act_own_kernel, "act_own_columns",
        (total_shape, pltpu.VMEM(acts.shape, acts.dtype), pltpu.VMEM(grad_factors.shape, grad_factors.dtype)),
        [IN_HBM] * 3,
        [pltpu.VMEM(act_factors.shape, act_factors.dtype), pltpu.SemaphoreType.DMA((3,))],
        ACT_OWN_MIB, acts.shape[1],
    )(in_hbm(acts), in_hbm(act_factors), in_hbm(grad_factors))
    later_factors, other_act, act_total = lax.optimization_barrier((grad_factors, other_act, act_total))
    other_grad = from_partner(later_factors, "loop", 1)
    (grad_total,) = kernel(
        grad_own_kernel, "grad_own_columns", (total_shape,), [IN_VMEM] * 2, [], 8, depth,
    )(in_vmem(grads), in_vmem(factor_held))
    own, *outs = kernel(
        act_other_kernel, "act_other_columns", (own_shape(3), *out_shapes(3)), [IN_VMEM] * 4, [total_shape],
        8, acts.shape[1],
    )(in_vmem(act_held), in_vmem(other_act), in_vmem(act_total), in_vmem(grad_total))
    own_in = to_quarters(outs)
    other, *outs = kernel(
        grad_other_kernel, "grad_other_columns", (own_shape(1), *out_shapes(1)), [IN_VMEM] * 2, [total_shape],
        8, depth,
    )(in_vmem(grads), in_vmem(other_grad))
    other_in = to_quarters(outs)
    seq_part = seq_dev // QUARTERS
    before, act_other = kernel(
        own_score_kernel, "own_scores", (score_shape, own_shape(1)), [IN_SMEM] + [IN_VMEM] * 4, [], 8, 0,
    )(lengths, in_vmem(own), *own_in)
    (total,) = kernel(
        functools.partial(other_score_kernel, seq_part), "other_scores", (score_shape,), [IN_VMEM] * 6, [], 8, 0,
    )(in_vmem(act_other), in_vmem(before), in_vmem(other), *other_in)

    total = total + from_partner(total, "loop", 1)
    gathered = [from_partner(total, both, mask * loop_count + 1) for mask in range(1, QUARTERS)]
    total = total + gathered[0] + gathered[1] + gathered[2]
    mask = QUARTERS
    while mask < layer_count:
        total = total + from_partner(total, both, mask * loop_count + 1)
        mask *= 2
    return total[:, :queries]


def solution(mesh):
    in_specs = (
        P("layer", ("groups", "loop"), None),
        P("layer", ("groups", "loop"), None),
        P("layer", None, "loop"),
        P("layer", None, "loop"),
        P(("groups", "loop")),
    )
    out_specs = P("groups", None)
    return jax.shard_map(
        on_device, mesh=mesh, in_specs=in_specs, out_specs=out_specs, check_vma=False
    )
```

```python
import functools

import jax
import jax.numpy as jnp
from jax import lax
from jax.experimental import pallas as pl
from jax.experimental.pallas import tpu as pltpu
from jax.sharding import PartitionSpec as P

RANK = 32
QUARTERS = 4
LANES = 128
SUBLANES = 16
TOP = 32000.0
STEPS = 256.0
FLOOR = 2.0**-112
MIB = 2**20
ACT_OWN_MIB = 50

IN_VMEM = pl.BlockSpec(memory_space=pltpu.VMEM)
IN_HBM = pl.BlockSpec(memory_space=pltpu.HBM)
IN_SMEM = pl.BlockSpec(memory_space=pltpu.SMEM)


def in_vmem(value):
    return pltpu.with_memory_space_constraint(value, pltpu.VMEM)


def in_hbm(value):
    return pltpu.with_memory_space_constraint(value, pltpu.HBM)


def from_partner(value, axis, mask):
    pairs = [(source, source ^ mask) for source in range(lax.axis_size(axis))]
    return lax.ppermute(value, axis, pairs)


def dot(rows, factor):
    return jnp.dot(rows, factor, preferred_element_type=jnp.float32)


def blocks(rows, width):
    return [
        (lane * (rows // SUBLANES) + row, row * SUBLANES, lane * LANES)
        for lane in range(width // LANES)
        for row in range(rows // SUBLANES)
    ]


def encode(part, out, codes, first):
    rows, width = part.shape
    peak = jnp.max(jnp.abs(part), axis=0, keepdims=True)
    code = jnp.ceil(jnp.log2(jnp.maximum(peak, FLOOR)) * STEPS) + 1.0
    fixed = jnp.round(part * (TOP * jnp.exp2(code * (-1.0 / STEPS))))
    fixed = fixed.astype(jnp.int32).astype(jnp.int16)
    lines, tiles = first // LANES, first // LANES * (rows // SUBLANES)
    for tile, row, lane in blocks(rows, width):
        out[tiles + tile] = fixed[row:row + SUBLANES, lane:lane + LANES]
    for index in range(width // LANES):
        codes[lines + index:lines + index + 1, :] = code[:, index * LANES:(index + 1) * LANES]


def received(own, messages, out):
    rows, width = own.shape
    last = messages[0].shape[0] - 1
    scales = [
        jnp.exp2(message[last].astype(jnp.int32).astype(jnp.float32) * (1.0 / STEPS)) * (1.0 / TOP)
        for message in messages
    ]
    for tile, row, lane in blocks(rows, width):
        here = (slice(row, row + SUBLANES), slice(lane, lane + LANES))
        line = lane // LANES
        full = own[here]
        for message, scale in zip(messages, scales):
            full = full + message[tile].astype(jnp.int32).astype(jnp.float32) * scale[line:line + 1, :]
        out[here] = full


def keep(part, total):
    rows = total.shape[1]
    for index in range(QUARTERS):
        total[index] = part[index * rows:(index + 1) * rows]


def share(parts, quarter, own, outs, codes):
    width = parts[0].shape[2]
    for index, part in enumerate(parts):
        own[:, index * width:(index + 1) * width] = part[quarter]
    for mask in range(1, QUARTERS):
        out = outs[mask - 1]
        codes[...] = jnp.zeros_like(codes)
        for index, part in enumerate(parts):
            encode(part[quarter ^ mask], out, codes, index * width)
        out[out.shape[0] - 1] = codes[...].astype(jnp.int32).astype(jnp.int16)


def act_own_kernel(acts, factor, grad_factor, total, rows_held, grad_factor_held, factor_held, sems):
    copies = (
        pltpu.make_async_copy(factor, factor_held, sems.at[0]),
        pltpu.make_async_copy(acts, rows_held, sems.at[1]),
        pltpu.make_async_copy(grad_factor, grad_factor_held, sems.at[2]),
    )
    for copy in copies:
        copy.start()
    copies[0].wait()
    copies[1].wait()
    keep(dot(rows_held[...], factor_held[...]), total)
    copies[2].wait()


def grad_own_kernel(grads, factor, total):
    keep(dot(grads[...], factor[...]), total)


def act_other_kernel(act_held, other_factor, act_total, grad_total, own, out1, out2, out3, total, codes):
    quarter = lax.axis_index("layer") % QUARTERS
    keep(dot(act_held[...], other_factor[...]), total)
    share((act_total, grad_total, total), quarter, own, (out1, out2, out3), codes)


def grad_other_kernel(grads, other_factor, own, out1, out2, out3, total, codes):
    quarter = lax.axis_index("layer") % QUARTERS
    keep(dot(grads[...], other_factor[...]), total)
    share((total,), quarter, own, (out1, out2, out3), codes)


def score(pair, seq_part, holder, out):
    quarter, position = lax.axis_index("layer") % QUARTERS, lax.axis_index("loop")
    rows, width = pair.shape
    pad_rows = rows // seq_part
    column = lax.broadcasted_iota(jnp.int32, (width, LANES), 0)
    lane = lax.broadcasted_iota(jnp.int32, (width, LANES), 1)
    pick = (lane == column // RANK + holder * (width // RANK)).astype(jnp.float32).astype(jnp.bfloat16)
    line = lax.broadcasted_iota(jnp.int32, out.shape, 0)
    result = jnp.zeros(out.shape, jnp.float32)
    for seq in range(seq_part):
        sums = jnp.sum(pair[seq * pad_rows:(seq + 1) * pad_rows], axis=0, keepdims=True)
        high = sums.astype(jnp.bfloat16).astype(jnp.float32)
        middle = (sums - high).astype(jnp.bfloat16).astype(jnp.float32)
        low = sums - high - middle
        term = lax.broadcasted_iota(jnp.int32, (8, width), 0)
        terms = jnp.where(term == 0, high, jnp.where(term == 1, middle, jnp.where(term == 2, low, 0.0)))
        scores = jnp.sum(dot(terms.astype(jnp.bfloat16), pick), axis=0, keepdims=True)
        at = (position * QUARTERS + quarter) * seq_part + seq
        result = result + jnp.where(line == at, scores, 0.0)
    return result


def own_score_kernel(lengths, own, in1, in2, in3, out, act_other, full):
    rows, width = act_other.shape
    seq_part = lengths.shape[0] // QUARTERS
    pad_rows = rows // seq_part
    quarter = lax.axis_index("layer") % QUARTERS
    received(own, (in1, in2, in3), full)
    offset = lax.broadcasted_iota(jnp.int32, (rows, width), 0)
    live = jnp.zeros((rows, width), jnp.bool_)
    for seq in range(seq_part):
        first = seq * pad_rows
        live = live | ((offset >= first) & (offset < first + lengths[quarter * seq_part + seq]))
    act_other[...] = jnp.where(live, full[:, 2 * width:], 0.0)
    pair = jnp.where(live, full[:, :width], 0.0) * full[:, width:2 * width]
    out[...] = score(pair, seq_part, lax.axis_index("loop"), out)


def other_score_kernel(seq_part, act_other, before, own, in1, in2, in3, out, full):
    received(own, (in1, in2, in3), full)
    pair = act_other[...] * full[...]
    out[...] = before[...] + score(pair, seq_part, 1 - lax.axis_index("loop"), out)


def on_device(acts, grads, act_factors, grad_factors, lengths):
    both = ("layer", "loop")
    loop_count = lax.axis_size("loop")
    layer_count = lax.axis_size("layer")
    acts, grads, act_factors, grad_factors = acts[0], grads[0], act_factors[0], grad_factors[0]
    seq_dev = lengths.shape[0]
    tok_rows, width = acts.shape[0], act_factors.shape[1]
    rows = tok_rows // QUARTERS
    queries = width * loop_count // RANK

    depth = grads.shape[1]

    def kernel(body, name, outs, specs, scratch, mib, work):
        return pl.pallas_call(
            body,
            name=name,
            out_shape=tuple(outs),
            in_specs=specs,
            out_specs=(IN_VMEM,) * len(outs),
            scratch_shapes=scratch,
            compiler_params=pltpu.CompilerParams(vmem_limit_bytes=mib * MIB),
            cost_estimate=pl.CostEstimate(
                flops=2 * tok_rows * width * work, bytes_accessed=mib * MIB, transcendentals=0
            ),
        )

    def own_shape(parts):
        return pltpu.VMEM((rows, parts * width), jnp.float32)

    def out_shapes(parts):
        tiles = (rows // SUBLANES) * (parts * width // LANES) + 1
        return [pltpu.VMEM((tiles, SUBLANES, LANES), jnp.int16)] * (QUARTERS - 1)

    def to_quarters(outs):
        return [in_vmem(from_partner(outs[mask - 1], "layer", mask)) for mask in (3, 2, 1)]

    total_shape = pltpu.VMEM((QUARTERS, rows, width), jnp.float32)
    codes_shape = pltpu.VMEM((SUBLANES, LANES), jnp.float32)
    score_shape = pltpu.VMEM((seq_dev * loop_count, LANES), jnp.float32)

    other_act = from_partner(act_factors, "loop", 1)
    act_total, act_held, factor_held = kernel(
        act_own_kernel, "act_own_columns",
        (total_shape, pltpu.VMEM(acts.shape, acts.dtype), pltpu.VMEM(grad_factors.shape, grad_factors.dtype)),
        [IN_HBM] * 3,
        [pltpu.VMEM(act_factors.shape, act_factors.dtype), pltpu.SemaphoreType.DMA((3,))],
        ACT_OWN_MIB, acts.shape[1],
    )(in_hbm(acts), in_hbm(act_factors), in_hbm(grad_factors))
    later_factors, other_act, act_total = lax.optimization_barrier((grad_factors, other_act, act_total))
    other_grad = from_partner(later_factors, "loop", 1)
    (grad_total,) = kernel(
        grad_own_kernel, "grad_own_columns", (total_shape,), [IN_VMEM] * 2, [], 8, depth,
    )(in_vmem(grads), in_vmem(factor_held))
    own, *outs = kernel(
        act_other_kernel, "act_other_columns", (own_shape(3), *out_shapes(3)), [IN_VMEM] * 4,
        [total_shape, codes_shape], 8, acts.shape[1],
    )(in_vmem(act_held), in_vmem(other_act), in_vmem(act_total), in_vmem(grad_total))
    own_in = to_quarters(outs)
    other, *outs = kernel(
        grad_other_kernel, "grad_other_columns", (own_shape(1), *out_shapes(1)), [IN_VMEM] * 2,
        [total_shape, codes_shape], 8, depth,
    )(in_vmem(grads), in_vmem(other_grad))
    other_in = to_quarters(outs)
    seq_part = seq_dev // QUARTERS
    before, act_other = kernel(
        own_score_kernel, "own_scores", (score_shape, own_shape(1)), [IN_SMEM] + [IN_VMEM] * 4, [own_shape(3)], 8, 0,
    )(lengths, in_vmem(own), *own_in)
    (total,) = kernel(
        functools.partial(other_score_kernel, seq_part), "other_scores", (score_shape,), [IN_VMEM] * 6,
        [own_shape(1)], 8, 0,
    )(in_vmem(act_other), in_vmem(before), in_vmem(other), *other_in)

    total = total + from_partner(total, "loop", 1)
    gathered = [from_partner(total, both, mask * loop_count + 1) for mask in range(1, QUARTERS)]
    total = total + gathered[0] + gathered[1] + gathered[2]
    mask = QUARTERS
    while mask < layer_count:
        total = total + from_partner(total, both, mask * loop_count + 1)
        mask *= 2
    return total[:, :queries]


def solution(mesh):
    in_specs = (
        P("layer", ("groups", "loop"), None),
        P("layer", ("groups", "loop"), None),
        P("layer", None, "loop"),
        P("layer", None, "loop"),
        P(("groups", "loop")),
    )
    out_specs = P("groups", None)
    return jax.shard_map(
        on_device, mesh=mesh, in_specs=in_specs, out_specs=out_specs, check_vma=False
    )
```

```python
import functools

import jax
import jax.numpy as jnp
from jax import lax
from jax.experimental import pallas as pl
from jax.experimental.pallas import tpu as pltpu
from jax.sharding import PartitionSpec as P

RANK = 32
QUARTERS = 4
LANES = 128
SUBLANES = 16
TOP = 32000.0
STEPS = 256.0
FLOOR = 2.0**-112
MIB = 2**20
ACT_OWN_MIB = 50

IN_VMEM = pl.BlockSpec(memory_space=pltpu.VMEM)
IN_HBM = pl.BlockSpec(memory_space=pltpu.HBM)
IN_SMEM = pl.BlockSpec(memory_space=pltpu.SMEM)


def in_vmem(value):
    return pltpu.with_memory_space_constraint(value, pltpu.VMEM)


def in_hbm(value):
    return pltpu.with_memory_space_constraint(value, pltpu.HBM)


def from_partner(value, axis, mask):
    pairs = [(source, source ^ mask) for source in range(lax.axis_size(axis))]
    return lax.ppermute(value, axis, pairs)


def dot(rows, factor):
    return jnp.dot(rows, factor, preferred_element_type=jnp.float32)


def blocks(rows, width):
    return [
        (lane * (rows // SUBLANES) + row, row * SUBLANES, lane * LANES)
        for lane in range(width // LANES)
        for row in range(rows // SUBLANES)
    ]


def blocks(rows, width):
    return [
        (lane * (rows // SUBLANES) + row, row * SUBLANES, lane * LANES)
        for lane in range(width // LANES)
        for row in range(rows // SUBLANES)
    ]


def encode(total, out, codes):
    count, rows, width = total.shape
    tiles, lines = (rows // SUBLANES) * (width // LANES), width // LANES
    codes[...] = jnp.zeros_like(codes)
    for index in range(count):
        part = total[index]
        peak = jnp.max(jnp.abs(part), axis=0, keepdims=True)
        code = jnp.ceil(jnp.log2(jnp.maximum(peak, FLOOR)) * STEPS) + 1.0
        fixed = jnp.round(part * (TOP * jnp.exp2(code * (-1.0 / STEPS))))
        fixed = fixed.astype(jnp.int32).astype(jnp.int16)
        for tile, row, lane in blocks(rows, width):
            out[index * tiles + tile] = fixed[row:row + SUBLANES, lane:lane + LANES]
        for line in range(lines):
            at = index * lines + line
            codes[at:at + 1, :] = code[:, line * LANES:(line + 1) * LANES]
    out[count * tiles] = codes[...].astype(jnp.int32).astype(jnp.int16)


def add(total, message, out):
    count, rows, width = total.shape
    tiles, lines = (rows // SUBLANES) * (width // LANES), width // LANES
    codes = message[count * tiles].astype(jnp.int32).astype(jnp.float32)
    scale = jnp.exp2(codes * (1.0 / STEPS)) * (1.0 / TOP)
    for index in range(count):
        for tile, row, lane in blocks(rows, width):
            here = (index, slice(row, row + SUBLANES), slice(lane, lane + LANES))
            line = index * lines + lane // LANES
            fixed = message[index * tiles + tile].astype(jnp.int32).astype(jnp.float32)
            out[here] = total[here] + fixed * scale[line:line + 1, :]


def keep(part, total):
    rows = total.shape[1]
    for index in range(total.shape[0]):
        total[index] = part[index * rows:(index + 1) * rows]


def act_own_kernel(acts, factor, grad_factor, total, out, rows_held, grad_factor_held, factor_held, codes, sems):
    copies = (
        pltpu.make_async_copy(factor, factor_held, sems.at[0]),
        pltpu.make_async_copy(acts, rows_held, sems.at[1]),
        pltpu.make_async_copy(grad_factor, grad_factor_held, sems.at[2]),
    )
    for copy in copies:
        copy.start()
    copies[0].wait()
    copies[1].wait()
    keep(dot(rows_held[...], factor_held[...]), total)
    encode(total, out, codes)
    copies[2].wait()


def act_other_kernel(rows_held, factor, total, out, codes):
    keep(dot(rows_held[...], factor[...]), total)
    encode(total, out, codes)


def pair_kernel(total, message, *refs):
    pair_total, out, codes = refs[-3:]
    add(total, message, pair_total)
    encode(pair_total, out, codes)


def grad_kernel(lengths, grads, factor, total):
    keep(dot(grads[...], factor[...]), total)
    offsets = lax.broadcasted_iota(jnp.int32, total.shape[1:], 0)
    for seq in range(total.shape[0]):
        total[seq] = jnp.where(offsets < lengths[seq], total[seq], 0.0)


def score_kernel(is_own, act_total, message, grad_total, before, out, act):
    add(act_total, message, act)
    position = lax.axis_index("loop")
    holder = position if is_own else 1 - position
    count, rows, width = act.shape
    column = lax.broadcasted_iota(jnp.int32, (width, LANES), 0)
    lane = lax.broadcasted_iota(jnp.int32, (width, LANES), 1)
    pick = (lane == column // RANK + holder * (width // RANK)).astype(jnp.float32).astype(jnp.bfloat16)
    line = lax.broadcasted_iota(jnp.int32, (8, LANES), 0)
    term = lax.broadcasted_iota(jnp.int32, (8, width), 0)
    for first in range(0, out.shape[0], 8):
        result = jnp.zeros((8, LANES), jnp.float32) if is_own else before[first:first + 8, :]
        high = middle = low = jnp.zeros((8, width), jnp.float32)
        for seq in range(count):
            sums = jnp.sum(act[seq] * grad_total[seq], axis=0, keepdims=True)
            here = term == position * count + seq - first
            high_part = sums.astype(jnp.bfloat16).astype(jnp.float32)
            middle_part = (sums - high_part).astype(jnp.bfloat16).astype(jnp.float32)
            high = jnp.where(here, high_part, high)
            middle = jnp.where(here, middle_part, middle)
            low = jnp.where(here, sums - high_part - middle_part, low)
        terms = jnp.concatenate([high, middle, low], axis=0).astype(jnp.bfloat16)
        scores = dot(terms, pick)
        out[first:first + 8, :] = result + scores[:8] + scores[8:16] + scores[16:]


def on_device(acts, grads, act_factors, grad_factors, lengths):
    both = ("layer", "loop")
    loop_count = lax.axis_size("loop")
    layer_count = lax.axis_size("layer")
    acts, grads, act_factors, grad_factors = acts[0], grads[0], act_factors[0], grad_factors[0]
    seq_dev = lengths.shape[0]
    tok_rows, width = acts.shape[0], act_factors.shape[1]
    pad_rows = tok_rows // seq_dev
    queries = width * loop_count // RANK

    depth = grads.shape[1]

    def kernel(body, name, outs, specs, scratch, mib, work):
        return pl.pallas_call(
            body,
            name=name,
            out_shape=tuple(outs),
            in_specs=specs,
            out_specs=(IN_VMEM,) * len(outs),
            scratch_shapes=scratch,
            compiler_params=pltpu.CompilerParams(vmem_limit_bytes=mib * MIB),
            cost_estimate=pl.CostEstimate(
                flops=2 * tok_rows * width * work, bytes_accessed=mib * MIB, transcendentals=0
            ),
        )

    seqs_shape = pltpu.VMEM((seq_dev, pad_rows, width), jnp.float32)
    codes_shape = pltpu.VMEM((SUBLANES, LANES), jnp.float32)
    score_shape = pltpu.VMEM((seq_dev * loop_count, LANES), jnp.float32)
    tiles = (tok_rows // SUBLANES) * (width // LANES) + 1
    message_shape = pltpu.VMEM((tiles, SUBLANES, LANES), jnp.int16)

    def to_pair(out, step):
        pairs = [
            (source * loop_count + core, (source ^ (1 << (core ^ step))) * loop_count + core)
            for source in range(layer_count)
            for core in range(loop_count)
        ]
        return in_vmem(lax.ppermute(out, both, pairs))

    other_act = from_partner(act_factors, "loop", 1)
    own_total, own_out, act_held, factor_held = kernel(
        act_own_kernel, "act_own_columns",
        (
            seqs_shape, message_shape, pltpu.VMEM(acts.shape, acts.dtype),
            pltpu.VMEM(grad_factors.shape, grad_factors.dtype),
        ),
        [IN_HBM] * 3,
        [pltpu.VMEM(act_factors.shape, act_factors.dtype), codes_shape, pltpu.SemaphoreType.DMA((3,))],
        ACT_OWN_MIB, acts.shape[1],
    )(in_hbm(acts), in_hbm(act_factors), in_hbm(grad_factors))
    own_in = to_pair(own_out, 0)
    later_factors, other_act, own_total = lax.optimization_barrier((grad_factors, other_act, own_total))
    other_grad = from_partner(later_factors, "loop", 1)
    other_total, other_out = kernel(
        act_other_kernel, "act_other_columns", (seqs_shape, message_shape), [IN_VMEM] * 2, [codes_shape],
        8, acts.shape[1],
    )(in_vmem(act_held), in_vmem(other_act))
    other_in = to_pair(other_out, 0)
    (grad_own,) = kernel(
        grad_kernel, "grad_own_columns", (seqs_shape,), [IN_SMEM] + [IN_VMEM] * 2, [], 8, depth,
    )(lengths, in_vmem(grads), in_vmem(factor_held))
    own_pair, own_out = kernel(
        pair_kernel, "own_pair", (seqs_shape, message_shape), [IN_VMEM] * 3, [codes_shape], 8, 0,
    )(in_vmem(own_total), own_in, in_vmem(grad_own))
    own_in = to_pair(own_out, 1)
    other_pair, other_out = kernel(
        pair_kernel, "other_pair", (seqs_shape, message_shape), [IN_VMEM] * 2, [codes_shape], 8, 0,
    )(in_vmem(other_total), other_in)
    other_in = to_pair(other_out, 1)
    (grad_other,) = kernel(
        grad_kernel, "grad_other_columns", (seqs_shape,), [IN_SMEM] + [IN_VMEM] * 2, [], 8, depth,
    )(lengths, in_vmem(grads), in_vmem(other_grad))
    (own_scores,) = kernel(
        functools.partial(score_kernel, True), "own_scores", (score_shape,), [IN_VMEM] * 4, [seqs_shape], 8, 0,
    )(in_vmem(own_pair), own_in, in_vmem(grad_own), in_vmem(grad_other))
    (total,) = kernel(
        functools.partial(score_kernel, False), "other_scores", (score_shape,), [IN_VMEM] * 4, [seqs_shape], 8, 0,
    )(in_vmem(other_pair), other_in, in_vmem(grad_other), in_vmem(own_scores))

    total = total + from_partner(total, "loop", 1)
    gathered = [from_partner(total, both, mask * loop_count + 1) for mask in range(1, QUARTERS)]
    total = total + gathered[0] + gathered[1] + gathered[2]
    mask = QUARTERS
    while mask < layer_count:
        total = total + from_partner(total, both, mask * loop_count + 1)
        mask *= 2
    return total[:, :queries]


def solution(mesh):
    in_specs = (
        P("layer", ("groups", "loop"), None),
        P("layer", ("groups", "loop"), None),
        P("layer", None, "loop"),
        P("layer", None, "loop"),
        P(("groups", "loop")),
    )
    out_specs = P("groups", None)
    return jax.shard_map(
        on_device, mesh=mesh, in_specs=in_specs, out_specs=out_specs, check_vma=False
    )
```

```python
import functools

import jax
import jax.numpy as jnp
from jax import lax
from jax.experimental import pallas as pl
from jax.experimental.pallas import tpu as pltpu
from jax.sharding import PartitionSpec as P

RANK = 32
QUARTERS = 4
LANES = 128
SUBLANES = 16
TOP = 32000.0
STEPS = 256.0
FLOOR = 2.0**-112
MIB = 2**20
GRAD_STEP = 1
ACT_OWN_MIB = 50

IN_VMEM = pl.BlockSpec(memory_space=pltpu.VMEM)
IN_HBM = pl.BlockSpec(memory_space=pltpu.HBM)
IN_SMEM = pl.BlockSpec(memory_space=pltpu.SMEM)


def in_vmem(value):
    return pltpu.with_memory_space_constraint(value, pltpu.VMEM)


def in_hbm(value):
    return pltpu.with_memory_space_constraint(value, pltpu.HBM)


def from_partner(value, axis, mask):
    pairs = [(source, source ^ mask) for source in range(lax.axis_size(axis))]
    return lax.ppermute(value, axis, pairs)


def dot(rows, factor):
    return jnp.dot(rows, factor, preferred_element_type=jnp.float32)


def blocks(rows, width):
    return [
        (lane * (rows // SUBLANES) + row, row * SUBLANES, lane * LANES)
        for lane in range(width // LANES)
        for row in range(rows // SUBLANES)
    ]


def blocks(rows, width):
    return [
        (lane * (rows // SUBLANES) + row, row * SUBLANES, lane * LANES)
        for lane in range(width // LANES)
        for row in range(rows // SUBLANES)
    ]


def encode(total, out, codes):
    count, rows, width = total.shape
    tiles, lines = (rows // SUBLANES) * (width // LANES), width // LANES
    codes[...] = jnp.zeros_like(codes)
    for index in range(count):
        part = total[index]
        peak = jnp.max(jnp.abs(part), axis=0, keepdims=True)
        code = jnp.ceil(jnp.log2(jnp.maximum(peak, FLOOR)) * STEPS) + 1.0
        fixed = jnp.round(part * (TOP * jnp.exp2(code * (-1.0 / STEPS))))
        fixed = fixed.astype(jnp.int32).astype(jnp.int16)
        for tile, row, lane in blocks(rows, width):
            out[index * tiles + tile] = fixed[row:row + SUBLANES, lane:lane + LANES]
        for line in range(lines):
            at = index * lines + line
            codes[at:at + 1, :] = code[:, line * LANES:(line + 1) * LANES]
    out[count * tiles] = codes[...].astype(jnp.int32).astype(jnp.int16)


def add(total, message, out):
    count, rows, width = total.shape
    tiles, lines = (rows // SUBLANES) * (width // LANES), width // LANES
    codes = message[count * tiles].astype(jnp.int32).astype(jnp.float32)
    scale = jnp.exp2(codes * (1.0 / STEPS)) * (1.0 / TOP)
    for index in range(count):
        for tile, row, lane in blocks(rows, width):
            here = (index, slice(row, row + SUBLANES), slice(lane, lane + LANES))
            line = index * lines + lane // LANES
            fixed = message[index * tiles + tile].astype(jnp.int32).astype(jnp.float32)
            out[here] = total[here] + fixed * scale[line:line + 1, :]


def keep(part, total):
    rows = total.shape[1]
    for index in range(total.shape[0]):
        total[index] = part[index * rows:(index + 1) * rows]


def act_own_kernel(acts, factor, grad_factor, total, out, rows_held, grad_factor_held, factor_held, codes, sems):
    copies = (
        pltpu.make_async_copy(factor, factor_held, sems.at[0]),
        pltpu.make_async_copy(acts, rows_held, sems.at[1]),
        pltpu.make_async_copy(grad_factor, grad_factor_held, sems.at[2]),
    )
    for copy in copies:
        copy.start()
    copies[0].wait()
    copies[1].wait()
    keep(dot(rows_held[...], factor_held[...]), total)
    encode(total, out, codes)
    copies[2].wait()


def act_other_kernel(rows_held, factor, total, out, codes):
    keep(dot(rows_held[...], factor[...]), total)
    encode(total, out, codes)


def pair_kernel(total, message, *refs):
    pair_total, out, codes = refs[-3:]
    add(total, message, pair_total)
    encode(pair_total, out, codes)


def grad_own_kernel(grads, factor, total, out, codes):
    keep(dot(grads[...], factor[...]), total)
    encode(total, out, codes)


def drop_padding(total, lengths):
    offsets = lax.broadcasted_iota(jnp.int32, total.shape[1:], 0)
    for seq in range(total.shape[0]):
        total[seq] = jnp.where(offsets < lengths[seq], total[seq], 0.0)


def grad_other_kernel(lengths, grads, factor, total):
    keep(dot(grads[...], factor[...]), total)
    drop_padding(total, lengths)


def score(act, grad, holder, out, before):
    position = lax.axis_index("loop")
    count, rows, width = act.shape
    column = lax.broadcasted_iota(jnp.int32, (width, LANES), 0)
    lane = lax.broadcasted_iota(jnp.int32, (width, LANES), 1)
    pick = (lane == column // RANK + holder * (width // RANK)).astype(jnp.float32).astype(jnp.bfloat16)
    term = lax.broadcasted_iota(jnp.int32, (8, width), 0)
    for first in range(0, out.shape[0], 8):
        high = middle = low = jnp.zeros((8, width), jnp.float32)
        for seq in range(count):
            sums = jnp.sum(act[seq] * grad[seq], axis=0, keepdims=True)
            here = term == position * count + seq - first
            high_part = sums.astype(jnp.bfloat16).astype(jnp.float32)
            middle_part = (sums - high_part).astype(jnp.bfloat16).astype(jnp.float32)
            high = jnp.where(here, high_part, high)
            middle = jnp.where(here, middle_part, middle)
            low = jnp.where(here, sums - high_part - middle_part, low)
        terms = jnp.concatenate([high, middle, low], axis=0).astype(jnp.bfloat16)
        scores = dot(terms, pick)
        scores = scores[:8] + scores[8:16] + scores[16:]
        out[first:first + 8, :] = scores if before is None else before[first:first + 8, :] + scores


def own_score_kernel(lengths, act_total, act_message, grad_total, grad_message, after, out, act, grad):
    add(act_total, act_message, act)
    add(grad_total, grad_message, grad)
    drop_padding(act, lengths)
    score(act, grad, lax.axis_index("loop"), out, None)


def other_score_kernel(act_total, message, grad_total, before, out, act):
    add(act_total, message, act)
    score(act, grad_total, 1 - lax.axis_index("loop"), out, before)


def on_device(acts, grads, act_factors, grad_factors, lengths):
    both = ("layer", "loop")
    loop_count = lax.axis_size("loop")
    layer_count = lax.axis_size("layer")
    acts, grads, act_factors, grad_factors = acts[0], grads[0], act_factors[0], grad_factors[0]
    seq_dev = lengths.shape[0]
    tok_rows, width = acts.shape[0], act_factors.shape[1]
    pad_rows = tok_rows // seq_dev
    queries = width * loop_count // RANK

    depth = grads.shape[1]

    def kernel(body, name, outs, specs, scratch, mib, work):
        return pl.pallas_call(
            body,
            name=name,
            out_shape=tuple(outs),
            in_specs=specs,
            out_specs=(IN_VMEM,) * len(outs),
            scratch_shapes=scratch,
            compiler_params=pltpu.CompilerParams(vmem_limit_bytes=mib * MIB),
            cost_estimate=pl.CostEstimate(
                flops=2 * tok_rows * width * work, bytes_accessed=mib * MIB, transcendentals=0
            ),
        )

    seqs_shape = pltpu.VMEM((seq_dev, pad_rows, width), jnp.float32)
    codes_shape = pltpu.VMEM((SUBLANES, LANES), jnp.float32)
    score_shape = pltpu.VMEM((seq_dev * loop_count, LANES), jnp.float32)
    tiles = (tok_rows // SUBLANES) * (width // LANES) + 1
    message_shape = pltpu.VMEM((tiles, SUBLANES, LANES), jnp.int16)

    def to_pair(out, step):
        pairs = [
            (source * loop_count + core, (source ^ (1 << (core ^ step))) * loop_count + core)
            for source in range(layer_count)
            for core in range(loop_count)
        ]
        return in_vmem(lax.ppermute(out, both, pairs))

    other_act = from_partner(act_factors, "loop", 1)
    own_total, own_out, act_held, factor_held = kernel(
        act_own_kernel, "act_own_columns",
        (
            seqs_shape, message_shape, pltpu.VMEM(acts.shape, acts.dtype),
            pltpu.VMEM(grad_factors.shape, grad_factors.dtype),
        ),
        [IN_HBM] * 3,
        [pltpu.VMEM(act_factors.shape, act_factors.dtype), codes_shape, pltpu.SemaphoreType.DMA((3,))],
        ACT_OWN_MIB, acts.shape[1],
    )(in_hbm(acts), in_hbm(act_factors), in_hbm(grad_factors))
    own_in = to_pair(own_out, 1 - GRAD_STEP)
    later_factors, other_act, own_total = lax.optimization_barrier((grad_factors, other_act, own_total))
    other_grad = from_partner(later_factors, "loop", 1)
    other_total, other_out = kernel(
        act_other_kernel, "act_other_columns", (seqs_shape, message_shape), [IN_VMEM] * 2, [codes_shape],
        8, acts.shape[1],
    )(in_vmem(act_held), in_vmem(other_act))
    other_in = to_pair(other_out, 0)
    grad_own, grad_out = kernel(
        grad_own_kernel, "grad_own_columns", (seqs_shape, message_shape), [IN_VMEM] * 2, [codes_shape], 8, depth,
    )(in_vmem(grads), in_vmem(factor_held))
    grad_in = to_pair(grad_out, GRAD_STEP)
    other_pair, other_out = kernel(
        pair_kernel, "other_pair", (seqs_shape, message_shape), [IN_VMEM] * 3, [codes_shape], 8, 0,
    )(in_vmem(other_total), other_in, in_vmem(grad_own))
    other_in = to_pair(other_out, 1)
    (grad_other,) = kernel(
        grad_other_kernel, "grad_other_columns", (seqs_shape,), [IN_SMEM] + [IN_VMEM] * 2, [], 8, depth,
    )(lengths, in_vmem(grads), in_vmem(other_grad))
    (own_scores,) = kernel(
        own_score_kernel, "own_scores", (score_shape,), [IN_SMEM] + [IN_VMEM] * 5, [seqs_shape] * 2, 8, 0,
    )(lengths, in_vmem(own_total), own_in, in_vmem(grad_own), grad_in, in_vmem(grad_other))
    (total,) = kernel(
        other_score_kernel, "other_scores", (score_shape,), [IN_VMEM] * 4, [seqs_shape], 8, 0,
    )(in_vmem(other_pair), other_in, in_vmem(grad_other), in_vmem(own_scores))

    total = total + from_partner(total, "loop", 1)
    gathered = [from_partner(total, both, mask * loop_count + 1) for mask in range(1, QUARTERS)]
    total = total + gathered[0] + gathered[1] + gathered[2]
    mask = QUARTERS
    while mask < layer_count:
        total = total + from_partner(total, both, mask * loop_count + 1)
        mask *= 2
    return total[:, :queries]


def solution(mesh):
    in_specs = (
        P("layer", ("groups", "loop"), None),
        P("layer", ("groups", "loop"), None),
        P("layer", None, "loop"),
        P("layer", None, "loop"),
        P(("groups", "loop")),
    )
    out_specs = P("groups", None)
    return jax.shard_map(
        on_device, mesh=mesh, in_specs=in_specs, out_specs=out_specs, check_vma=False
    )
```

```python
import functools

import jax
import jax.numpy as jnp
from jax import lax
from jax.experimental import pallas as pl
from jax.experimental.pallas import tpu as pltpu
from jax.sharding import PartitionSpec as P

RANK = 32
QUARTERS = 4
LANES = 128
SUBLANES = 16
TOP = 32000.0
STEPS = 256.0
FLOOR = 2.0**-112
MIB = 2**20
GRAD_STEP = 1
ACT_OWN_MIB = 16

IN_VMEM = pl.BlockSpec(memory_space=pltpu.VMEM)
IN_HBM = pl.BlockSpec(memory_space=pltpu.HBM)
IN_SMEM = pl.BlockSpec(memory_space=pltpu.SMEM)


def in_vmem(value):
    return pltpu.with_memory_space_constraint(value, pltpu.VMEM)


def in_hbm(value):
    return pltpu.with_memory_space_constraint(value, pltpu.HBM)


def from_partner(value, axis, mask):
    pairs = [(source, source ^ mask) for source in range(lax.axis_size(axis))]
    return lax.ppermute(value, axis, pairs)


def dot(rows, factor):
    return jnp.dot(rows, factor, preferred_element_type=jnp.float32)


def blocks(rows, width):
    return [
        (lane * (rows // SUBLANES) + row, row * SUBLANES, lane * LANES)
        for lane in range(width // LANES)
        for row in range(rows // SUBLANES)
    ]


def blocks(rows, width):
    return [
        (lane * (rows // SUBLANES) + row, row * SUBLANES, lane * LANES)
        for lane in range(width // LANES)
        for row in range(rows // SUBLANES)
    ]


def encode(total, out, codes):
    count, rows, width = total.shape
    tiles, lines = (rows // SUBLANES) * (width // LANES), width // LANES
    codes[...] = jnp.zeros_like(codes)
    for index in range(count):
        part = total[index]
        peak = jnp.max(jnp.abs(part), axis=0, keepdims=True)
        code = jnp.ceil(jnp.log2(jnp.maximum(peak, FLOOR)) * STEPS) + 1.0
        fixed = jnp.round(part * (TOP * jnp.exp2(code * (-1.0 / STEPS))))
        fixed = fixed.astype(jnp.int32).astype(jnp.int16)
        for tile, row, lane in blocks(rows, width):
            out[index * tiles + tile] = fixed[row:row + SUBLANES, lane:lane + LANES]
        for line in range(lines):
            at = index * lines + line
            codes[at:at + 1, :] = code[:, line * LANES:(line + 1) * LANES]
    out[count * tiles] = codes[...].astype(jnp.int32).astype(jnp.int16)


def add(total, message, out):
    count, rows, width = total.shape
    tiles, lines = (rows // SUBLANES) * (width // LANES), width // LANES
    codes = message[count * tiles].astype(jnp.int32).astype(jnp.float32)
    scale = jnp.exp2(codes * (1.0 / STEPS)) * (1.0 / TOP)
    for index in range(count):
        for tile, row, lane in blocks(rows, width):
            here = (index, slice(row, row + SUBLANES), slice(lane, lane + LANES))
            line = index * lines + lane // LANES
            fixed = message[index * tiles + tile].astype(jnp.int32).astype(jnp.float32)
            out[here] = total[here] + fixed * scale[line:line + 1, :]


def keep(part, total):
    rows = total.shape[1]
    for index in range(total.shape[0]):
        total[index] = part[index * rows:(index + 1) * rows]


def act_own_kernel(acts, factor, grad_factor, total, out, rows_held, grad_factor_held, factor_held, codes, sems):
    copies = (
        pltpu.make_async_copy(factor, factor_held, sems.at[0]),
        pltpu.make_async_copy(acts, rows_held, sems.at[1]),
        pltpu.make_async_copy(grad_factor, grad_factor_held, sems.at[2]),
    )
    for copy in copies:
        copy.start()
    copies[0].wait()
    copies[1].wait()
    keep(dot(rows_held[...], factor_held[...]), total)
    encode(total, out, codes)
    copies[2].wait()


def act_other_kernel(rows_held, factor, total, out, codes):
    keep(dot(rows_held[...], factor[...]), total)
    encode(total, out, codes)


def pair_kernel(total, message, *refs):
    pair_total, out, codes = refs[-3:]
    add(total, message, pair_total)
    encode(pair_total, out, codes)


def grad_own_kernel(grads, factor, total, out, codes):
    keep(dot(grads[...], factor[...]), total)
    encode(total, out, codes)


def drop_padding(total, lengths):
    offsets = lax.broadcasted_iota(jnp.int32, total.shape[1:], 0)
    for seq in range(total.shape[0]):
        total[seq] = jnp.where(offsets < lengths[seq], total[seq], 0.0)


def grad_other_kernel(lengths, grads, factor, total):
    keep(dot(grads[...], factor[...]), total)
    drop_padding(total, lengths)


def score(act, grad, holder, out, before):
    position = lax.axis_index("loop")
    count, rows, width = act.shape
    column = lax.broadcasted_iota(jnp.int32, (width, LANES), 0)
    lane = lax.broadcasted_iota(jnp.int32, (width, LANES), 1)
    pick = (lane == column // RANK + holder * (width // RANK)).astype(jnp.float32).astype(jnp.bfloat16)
    term = lax.broadcasted_iota(jnp.int32, (8, width), 0)
    for first in range(0, out.shape[0], 8):
        high = middle = low = jnp.zeros((8, width), jnp.float32)
        for seq in range(count):
            sums = jnp.sum(act[seq] * grad[seq], axis=0, keepdims=True)
            here = term == position * count + seq - first
            high_part = sums.astype(jnp.bfloat16).astype(jnp.float32)
            middle_part = (sums - high_part).astype(jnp.bfloat16).astype(jnp.float32)
            high = jnp.where(here, high_part, high)
            middle = jnp.where(here, middle_part, middle)
            low = jnp.where(here, sums - high_part - middle_part, low)
        terms = jnp.concatenate([high, middle, low], axis=0).astype(jnp.bfloat16)
        scores = dot(terms, pick)
        scores = scores[:8] + scores[8:16] + scores[16:]
        out[first:first + 8, :] = scores if before is None else before[first:first + 8, :] + scores


def own_score_kernel(lengths, act_total, act_message, grad_total, grad_message, after, out, act, grad):
    add(act_total, act_message, act)
    add(grad_total, grad_message, grad)
    drop_padding(act, lengths)
    score(act, grad, lax.axis_index("loop"), out, None)


def other_score_kernel(act_total, message, grad_total, before, out, act):
    add(act_total, message, act)
    score(act, grad_total, 1 - lax.axis_index("loop"), out, before)


def on_device(acts, grads, act_factors, grad_factors, lengths):
    both = ("layer", "loop")
    loop_count = lax.axis_size("loop")
    layer_count = lax.axis_size("layer")
    acts, grads, act_factors, grad_factors = acts[0], grads[0], act_factors[0], grad_factors[0]
    seq_dev = lengths.shape[0]
    tok_rows, width = acts.shape[0], act_factors.shape[1]
    pad_rows = tok_rows // seq_dev
    queries = width * loop_count // RANK

    depth = grads.shape[1]

    def kernel(body, name, outs, specs, scratch, mib, work):
        return pl.pallas_call(
            body,
            name=name,
            out_shape=tuple(outs),
            in_specs=specs,
            out_specs=(IN_VMEM,) * len(outs),
            scratch_shapes=scratch,
            compiler_params=pltpu.CompilerParams(vmem_limit_bytes=mib * MIB),
            cost_estimate=pl.CostEstimate(
                flops=2 * tok_rows * width * work, bytes_accessed=mib * MIB, transcendentals=0
            ),
        )

    seqs_shape = pltpu.VMEM((seq_dev, pad_rows, width), jnp.float32)
    codes_shape = pltpu.VMEM((SUBLANES, LANES), jnp.float32)
    score_shape = pltpu.VMEM((seq_dev * loop_count, LANES), jnp.float32)
    tiles = (tok_rows // SUBLANES) * (width // LANES) + 1
    message_shape = pltpu.VMEM((tiles, SUBLANES, LANES), jnp.int16)

    def to_pair(out, step):
        pairs = [
            (source * loop_count + core, (source ^ (1 << (core ^ step))) * loop_count + core)
            for source in range(layer_count)
            for core in range(loop_count)
        ]
        return in_vmem(lax.ppermute(out, both, pairs))

    other_act = from_partner(act_factors, "loop", 1)
    own_total, own_out, act_held, factor_held = kernel(
        act_own_kernel, "act_own_columns",
        (
            seqs_shape, message_shape, pltpu.VMEM(acts.shape, acts.dtype),
            pltpu.VMEM(grad_factors.shape, grad_factors.dtype),
        ),
        [IN_HBM] * 3,
        [pltpu.VMEM(act_factors.shape, act_factors.dtype), codes_shape, pltpu.SemaphoreType.DMA((3,))],
        ACT_OWN_MIB, acts.shape[1],
    )(in_hbm(acts), in_hbm(act_factors), in_hbm(grad_factors))
    own_in = to_pair(own_out, 1 - GRAD_STEP)
    later_factors, other_act, own_total = lax.optimization_barrier((grad_factors, other_act, own_total))
    other_grad = from_partner(later_factors, "loop", 1)
    other_total, other_out = kernel(
        act_other_kernel, "act_other_columns", (seqs_shape, message_shape), [IN_VMEM] * 2, [codes_shape],
        8, acts.shape[1],
    )(in_vmem(act_held), in_vmem(other_act))
    other_in = to_pair(other_out, 0)
    grad_own, grad_out = kernel(
        grad_own_kernel, "grad_own_columns", (seqs_shape, message_shape), [IN_VMEM] * 2, [codes_shape], 16, depth,
    )(in_vmem(grads), in_vmem(factor_held))
    grad_in = to_pair(grad_out, GRAD_STEP)
    other_pair, other_out = kernel(
        pair_kernel, "other_pair", (seqs_shape, message_shape), [IN_VMEM] * 3, [codes_shape], 8, 0,
    )(in_vmem(other_total), other_in, in_vmem(grad_own))
    other_in = to_pair(other_out, 1)
    (grad_other,) = kernel(
        grad_other_kernel, "grad_other_columns", (seqs_shape,), [IN_SMEM] + [IN_VMEM] * 2, [], 16, depth,
    )(lengths, in_vmem(grads), in_vmem(other_grad))
    (own_scores,) = kernel(
        own_score_kernel, "own_scores", (score_shape,), [IN_SMEM] + [IN_VMEM] * 5, [seqs_shape] * 2, 8, 0,
    )(lengths, in_vmem(own_total), own_in, in_vmem(grad_own), grad_in, in_vmem(grad_other))
    (total,) = kernel(
        other_score_kernel, "other_scores", (score_shape,), [IN_VMEM] * 4, [seqs_shape], 8, 0,
    )(in_vmem(other_pair), other_in, in_vmem(grad_other), in_vmem(own_scores))

    total = total + from_partner(total, "loop", 1)
    gathered = [from_partner(total, both, mask * loop_count + 1) for mask in range(1, QUARTERS)]
    total = total + gathered[0] + gathered[1] + gathered[2]
    mask = QUARTERS
    while mask < layer_count:
        total = total + from_partner(total, both, mask * loop_count + 1)
        mask *= 2
    return total[:, :queries]


def solution(mesh):
    in_specs = (
        P("layer", ("groups", "loop"), None),
        P("layer", ("groups", "loop"), None),
        P("layer", None, "loop"),
        P("layer", None, "loop"),
        P(("groups", "loop")),
    )
    out_specs = P("groups", None)
    return jax.shard_map(
        on_device, mesh=mesh, in_specs=in_specs, out_specs=out_specs, check_vma=False
    )
```

```python
import functools

import jax
import jax.numpy as jnp
from jax import lax
from jax.experimental import pallas as pl
from jax.experimental.pallas import tpu as pltpu
from jax.sharding import PartitionSpec as P

RANK = 32
QUARTERS = 4
LANES = 128
SUBLANES = 16
TOP = 32000.0
STEPS = 256.0
FLOOR = 2.0**-112
MIB = 2**20
GRAD_STEP = 1
ACT_OWN_MIB = 16

IN_VMEM = pl.BlockSpec(memory_space=pltpu.VMEM)
IN_HBM = pl.BlockSpec(memory_space=pltpu.HBM)
IN_SMEM = pl.BlockSpec(memory_space=pltpu.SMEM)


def in_vmem(value):
    return pltpu.with_memory_space_constraint(value, pltpu.VMEM)


def in_hbm(value):
    return pltpu.with_memory_space_constraint(value, pltpu.HBM)


def from_partner(value, axis, mask):
    pairs = [(source, source ^ mask) for source in range(lax.axis_size(axis))]
    return lax.ppermute(value, axis, pairs)


def dot(rows, factor):
    return jnp.dot(rows, factor, preferred_element_type=jnp.float32)


def blocks(rows, width):
    return [
        (lane * (rows // SUBLANES) + row, row * SUBLANES, lane * LANES)
        for lane in range(width // LANES)
        for row in range(rows // SUBLANES)
    ]


def blocks(rows, width):
    return [
        (lane * (rows // SUBLANES) + row, row * SUBLANES, lane * LANES)
        for lane in range(width // LANES)
        for row in range(rows // SUBLANES)
    ]


def encode(total, out, codes):
    count, rows, width = total.shape
    tiles, lines = (rows // SUBLANES) * (width // LANES), width // LANES
    codes[...] = jnp.zeros_like(codes)
    for index in range(count):
        part = total[index]
        peak = jnp.max(jnp.abs(part), axis=0, keepdims=True)
        code = jnp.ceil(jnp.log2(jnp.maximum(peak, FLOOR)) * STEPS) + 1.0
        fixed = jnp.round(part * (TOP * jnp.exp2(code * (-1.0 / STEPS))))
        fixed = fixed.astype(jnp.int32).astype(jnp.int16)
        for tile, row, lane in blocks(rows, width):
            out[index * tiles + tile] = fixed[row:row + SUBLANES, lane:lane + LANES]
        for line in range(lines):
            at = index * lines + line
            codes[at:at + 1, :] = code[:, line * LANES:(line + 1) * LANES]
    out[count * tiles] = codes[...].astype(jnp.int32).astype(jnp.int16)


def add(total, message, out):
    count, rows, width = total.shape
    tiles, lines = (rows // SUBLANES) * (width // LANES), width // LANES
    codes = message[count * tiles].astype(jnp.int32).astype(jnp.float32)
    scale = jnp.exp2(codes * (1.0 / STEPS)) * (1.0 / TOP)
    for index in range(count):
        for tile, row, lane in blocks(rows, width):
            here = (index, slice(row, row + SUBLANES), slice(lane, lane + LANES))
            line = index * lines + lane // LANES
            fixed = message[index * tiles + tile].astype(jnp.int32).astype(jnp.float32)
            out[here] = total[here] + fixed * scale[line:line + 1, :]


def keep(part, total):
    rows = total.shape[1]
    for index in range(total.shape[0]):
        total[index] = part[index * rows:(index + 1) * rows]


def act_own_kernel(acts, factor, grad_factor, total, out, rows_held, grad_factor_held, factor_held, codes, sems):
    copies = (
        pltpu.make_async_copy(factor, factor_held, sems.at[0]),
        pltpu.make_async_copy(acts, rows_held, sems.at[1]),
        pltpu.make_async_copy(grad_factor, grad_factor_held, sems.at[2]),
    )
    for copy in copies:
        copy.start()
    copies[0].wait()
    copies[1].wait()
    keep(dot(rows_held[...], factor_held[...]), total)
    encode(total, out, codes)
    copies[2].wait()


def act_other_kernel(rows_held, factor, total, out, codes):
    keep(dot(rows_held[...], factor[...]), total)
    encode(total, out, codes)


def pair_kernel(total, message, *refs):
    pair_total, out, codes = refs[-3:]
    add(total, message, pair_total)
    encode(pair_total, out, codes)


def grad_own_kernel(grads, factor, total, out, codes):
    keep(dot(grads[...], factor[...]), total)
    encode(total, out, codes)


def drop_padding(total, lengths):
    offsets = lax.broadcasted_iota(jnp.int32, total.shape[1:], 0)
    for seq in range(total.shape[0]):
        total[seq] = jnp.where(offsets < lengths[seq], total[seq], 0.0)


def grad_other_kernel(grads, factor, total):
    keep(dot(grads[...], factor[...]), total)


def score(act, grad, holder, out, before):
    position = lax.axis_index("loop")
    count, rows, width = act.shape
    column = lax.broadcasted_iota(jnp.int32, (width, LANES), 0)
    lane = lax.broadcasted_iota(jnp.int32, (width, LANES), 1)
    pick = (lane == column // RANK + holder * (width // RANK)).astype(jnp.float32).astype(jnp.bfloat16)
    term = lax.broadcasted_iota(jnp.int32, (8, width), 0)
    for first in range(0, out.shape[0], 8):
        high = middle = low = jnp.zeros((8, width), jnp.float32)
        for seq in range(count):
            sums = jnp.sum(act[seq] * grad[seq], axis=0, keepdims=True)
            here = term == position * count + seq - first
            high_part = sums.astype(jnp.bfloat16).astype(jnp.float32)
            middle_part = (sums - high_part).astype(jnp.bfloat16).astype(jnp.float32)
            high = jnp.where(here, high_part, high)
            middle = jnp.where(here, middle_part, middle)
            low = jnp.where(here, sums - high_part - middle_part, low)
        terms = jnp.concatenate([high, middle, low], axis=0).astype(jnp.bfloat16)
        scores = dot(terms, pick)
        scores = scores[:8] + scores[8:16] + scores[16:]
        out[first:first + 8, :] = scores if before is None else before[first:first + 8, :] + scores


def own_score_kernel(lengths, act_total, act_message, grad_total, grad_message, grad_other, out, live, act, grad):
    add(act_total, act_message, act)
    add(grad_total, grad_message, grad)
    drop_padding(act, lengths)
    live[...] = grad_other[...]
    drop_padding(live, lengths)
    score(act, grad, lax.axis_index("loop"), out, None)


def other_score_kernel(act_total, message, grad_total, before, out, act):
    add(act_total, message, act)
    score(act, grad_total, 1 - lax.axis_index("loop"), out, before)


def on_device(acts, grads, act_factors, grad_factors, lengths):
    both = ("layer", "loop")
    loop_count = lax.axis_size("loop")
    layer_count = lax.axis_size("layer")
    acts, grads, act_factors, grad_factors = acts[0], grads[0], act_factors[0], grad_factors[0]
    seq_dev = lengths.shape[0]
    tok_rows, width = acts.shape[0], act_factors.shape[1]
    pad_rows = tok_rows // seq_dev
    queries = width * loop_count // RANK

    depth = grads.shape[1]

    def kernel(body, name, outs, specs, scratch, mib, work):
        return pl.pallas_call(
            body,
            name=name,
            out_shape=tuple(outs),
            in_specs=specs,
            out_specs=(IN_VMEM,) * len(outs),
            scratch_shapes=scratch,
            compiler_params=pltpu.CompilerParams(vmem_limit_bytes=mib * MIB),
            cost_estimate=pl.CostEstimate(
                flops=2 * tok_rows * width * work, bytes_accessed=mib * MIB, transcendentals=0
            ),
        )

    seqs_shape = pltpu.VMEM((seq_dev, pad_rows, width), jnp.float32)
    codes_shape = pltpu.VMEM((SUBLANES, LANES), jnp.float32)
    score_shape = pltpu.VMEM((seq_dev * loop_count, LANES), jnp.float32)
    tiles = (tok_rows // SUBLANES) * (width // LANES) + 1
    message_shape = pltpu.VMEM((tiles, SUBLANES, LANES), jnp.int16)

    def to_pair(out, step):
        pairs = [
            (source * loop_count + core, (source ^ (1 << (core ^ step))) * loop_count + core)
            for source in range(layer_count)
            for core in range(loop_count)
        ]
        return in_vmem(lax.ppermute(out, both, pairs))

    other_act = from_partner(act_factors, "loop", 1)
    own_total, own_out, act_held, factor_held = kernel(
        act_own_kernel, "act_own_columns",
        (
            seqs_shape, message_shape, pltpu.VMEM(acts.shape, acts.dtype),
            pltpu.VMEM(grad_factors.shape, grad_factors.dtype),
        ),
        [IN_HBM] * 3,
        [pltpu.VMEM(act_factors.shape, act_factors.dtype), codes_shape, pltpu.SemaphoreType.DMA((3,))],
        ACT_OWN_MIB, acts.shape[1],
    )(in_hbm(acts), in_hbm(act_factors), in_hbm(grad_factors))
    own_in = to_pair(own_out, 1 - GRAD_STEP)
    later_factors, other_act, own_total = lax.optimization_barrier((grad_factors, other_act, own_total))
    other_grad = from_partner(later_factors, "loop", 1)
    other_total, other_out = kernel(
        act_other_kernel, "act_other_columns", (seqs_shape, message_shape), [IN_VMEM] * 2, [codes_shape],
        8, acts.shape[1],
    )(in_vmem(act_held), in_vmem(other_act))
    other_in = to_pair(other_out, 0)
    grad_own, grad_out = kernel(
        grad_own_kernel, "grad_own_columns", (seqs_shape, message_shape), [IN_VMEM] * 2, [codes_shape], 16, depth,
    )(in_vmem(grads), in_vmem(factor_held))
    grad_in = to_pair(grad_out, GRAD_STEP)
    other_pair, other_out = kernel(
        pair_kernel, "other_pair", (seqs_shape, message_shape), [IN_VMEM] * 3, [codes_shape], 8, 0,
    )(in_vmem(other_total), other_in, in_vmem(grad_own))
    other_in = to_pair(other_out, 1)
    (grad_other,) = kernel(
        grad_other_kernel, "grad_other_columns", (seqs_shape,), [IN_VMEM] * 2, [], 16, depth,
    )(in_vmem(grads), in_vmem(other_grad))
    own_scores, grad_other = kernel(
        own_score_kernel, "own_scores", (score_shape, seqs_shape), [IN_SMEM] + [IN_VMEM] * 5, [seqs_shape] * 2, 8, 0,
    )(lengths, in_vmem(own_total), own_in, in_vmem(grad_own), grad_in, in_vmem(grad_other))
    (total,) = kernel(
        other_score_kernel, "other_scores", (score_shape,), [IN_VMEM] * 4, [seqs_shape], 8, 0,
    )(in_vmem(other_pair), other_in, in_vmem(grad_other), in_vmem(own_scores))

    total = total + from_partner(total, "loop", 1)
    gathered = [from_partner(total, both, mask * loop_count + 1) for mask in range(1, QUARTERS)]
    total = total + gathered[0] + gathered[1] + gathered[2]
    mask = QUARTERS
    while mask < layer_count:
        total = total + from_partner(total, both, mask * loop_count + 1)
        mask *= 2
    return total[:, :queries]


def solution(mesh):
    in_specs = (
        P("layer", ("groups", "loop"), None),
        P("layer", ("groups", "loop"), None),
        P("layer", None, "loop"),
        P("layer", None, "loop"),
        P(("groups", "loop")),
    )
    out_specs = P("groups", None)
    return jax.shard_map(
        on_device, mesh=mesh, in_specs=in_specs, out_specs=out_specs, check_vma=False
    )
```

```python
import functools

import jax
import jax.numpy as jnp
from jax import lax
from jax.experimental import pallas as pl
from jax.experimental.pallas import tpu as pltpu
from jax.sharding import PartitionSpec as P

RANK = 32
QUARTERS = 4
LANES = 128
SUBLANES = 16
TOP = 32000.0
STEPS = 256.0
FLOOR = 2.0**-112
MIB = 2**20
GRAD_STEP = 1
ACT_OWN_MIB = 16

IN_VMEM = pl.BlockSpec(memory_space=pltpu.VMEM)
IN_HBM = pl.BlockSpec(memory_space=pltpu.HBM)
IN_SMEM = pl.BlockSpec(memory_space=pltpu.SMEM)


def in_vmem(value):
    return pltpu.with_memory_space_constraint(value, pltpu.VMEM)


def in_hbm(value):
    return pltpu.with_memory_space_constraint(value, pltpu.HBM)


def from_partner(value, axis, mask):
    pairs = [(source, source ^ mask) for source in range(lax.axis_size(axis))]
    return lax.ppermute(value, axis, pairs)


def dot(rows, factor):
    return jnp.dot(rows, factor, preferred_element_type=jnp.float32)


def blocks(rows, width):
    return [
        (lane * (rows // SUBLANES) + row, row * SUBLANES, lane * LANES)
        for lane in range(width // LANES)
        for row in range(rows // SUBLANES)
    ]


def blocks(rows, width):
    return [
        (lane * (rows // SUBLANES) + row, row * SUBLANES, lane * LANES)
        for lane in range(width // LANES)
        for row in range(rows // SUBLANES)
    ]


def encode(total, out, codes):
    count, rows, width = total.shape
    tiles, lines = (rows // SUBLANES) * (width // LANES), width // LANES
    codes[...] = jnp.zeros_like(codes)
    for index in range(count):
        part = total[index]
        peak = jnp.max(jnp.abs(part), axis=0, keepdims=True)
        code = jnp.ceil(jnp.log2(jnp.maximum(peak, FLOOR)) * STEPS) + 1.0
        fixed = jnp.round(part * (TOP * jnp.exp2(code * (-1.0 / STEPS))))
        fixed = fixed.astype(jnp.int32).astype(jnp.int16)
        for tile, row, lane in blocks(rows, width):
            out[index * tiles + tile] = fixed[row:row + SUBLANES, lane:lane + LANES]
        for line in range(lines):
            at = index * lines + line
            codes[at:at + 1, :] = code[:, line * LANES:(line + 1) * LANES]
    out[count * tiles] = codes[...].astype(jnp.int32).astype(jnp.int16)


def add(total, message, out):
    count, rows, width = total.shape
    tiles, lines = (rows // SUBLANES) * (width // LANES), width // LANES
    codes = message[count * tiles].astype(jnp.int32).astype(jnp.float32)
    scale = jnp.exp2(codes * (1.0 / STEPS)) * (1.0 / TOP)
    for index in range(count):
        for tile, row, lane in blocks(rows, width):
            here = (index, slice(row, row + SUBLANES), slice(lane, lane + LANES))
            line = index * lines + lane // LANES
            fixed = message[index * tiles + tile].astype(jnp.int32).astype(jnp.float32)
            out[here] = total[here] + fixed * scale[line:line + 1, :]


def keep(part, total):
    rows = total.shape[1]
    for index in range(total.shape[0]):
        total[index] = part[index * rows:(index + 1) * rows]


def act_own_kernel(acts, factor, grad_factor, total, out, rows_held, grad_factor_held, factor_held, codes, sems):
    copies = []
    for source, held in ((factor, factor_held), (acts, rows_held), (grad_factor, grad_factor_held)):
        size = source.shape[0] // 2
        for index in range(2):
            span = pl.ds(index * size, size)
            copies.append(pltpu.make_async_copy(source.at[span, :], held.at[span, :], sems.at[len(copies)]))
            copies[-1].start()
    for copy in copies[:4]:
        copy.wait()
    keep(dot(rows_held[...], factor_held[...]), total)
    encode(total, out, codes)
    for copy in copies[4:]:
        copy.wait()


def act_other_kernel(rows_held, factor, total, out, codes):
    keep(dot(rows_held[...], factor[...]), total)
    encode(total, out, codes)


def pair_kernel(total, message, *refs):
    pair_total, out, codes = refs[-3:]
    add(total, message, pair_total)
    encode(pair_total, out, codes)


def grad_own_kernel(grads, factor, total, out, codes):
    keep(dot(grads[...], factor[...]), total)
    encode(total, out, codes)


def drop_padding(total, lengths):
    offsets = lax.broadcasted_iota(jnp.int32, total.shape[1:], 0)
    for seq in range(total.shape[0]):
        total[seq] = jnp.where(offsets < lengths[seq], total[seq], 0.0)


def grad_other_kernel(grads, factor, total):
    keep(dot(grads[...], factor[...]), total)


def score(act, grad, holder, out, before):
    position = lax.axis_index("loop")
    count, rows, width = act.shape
    column = lax.broadcasted_iota(jnp.int32, (width, LANES), 0)
    lane = lax.broadcasted_iota(jnp.int32, (width, LANES), 1)
    pick = (lane == column // RANK + holder * (width // RANK)).astype(jnp.float32).astype(jnp.bfloat16)
    term = lax.broadcasted_iota(jnp.int32, (8, width), 0)
    for first in range(0, out.shape[0], 8):
        high = middle = low = jnp.zeros((8, width), jnp.float32)
        for seq in range(count):
            sums = jnp.sum(act[seq] * grad[seq], axis=0, keepdims=True)
            here = term == position * count + seq - first
            high_part = sums.astype(jnp.bfloat16).astype(jnp.float32)
            middle_part = (sums - high_part).astype(jnp.bfloat16).astype(jnp.float32)
            high = jnp.where(here, high_part, high)
            middle = jnp.where(here, middle_part, middle)
            low = jnp.where(here, sums - high_part - middle_part, low)
        terms = jnp.concatenate([high, middle, low], axis=0).astype(jnp.bfloat16)
        scores = dot(terms, pick)
        scores = scores[:8] + scores[8:16] + scores[16:]
        out[first:first + 8, :] = scores if before is None else before[first:first + 8, :] + scores


def own_score_kernel(lengths, act_total, act_message, grad_total, grad_message, grad_other, out, live, act, grad):
    add(act_total, act_message, act)
    add(grad_total, grad_message, grad)
    drop_padding(act, lengths)
    live[...] = grad_other[...]
    drop_padding(live, lengths)
    score(act, grad, lax.axis_index("loop"), out, None)


def other_score_kernel(act_total, message, grad_total, before, out, act):
    add(act_total, message, act)
    score(act, grad_total, 1 - lax.axis_index("loop"), out, before)


def on_device(acts, grads, act_factors, grad_factors, lengths):
    both = ("layer", "loop")
    loop_count = lax.axis_size("loop")
    layer_count = lax.axis_size("layer")
    acts, grads, act_factors, grad_factors = acts[0], grads[0], act_factors[0], grad_factors[0]
    seq_dev = lengths.shape[0]
    tok_rows, width = acts.shape[0], act_factors.shape[1]
    pad_rows = tok_rows // seq_dev
    queries = width * loop_count // RANK

    depth = grads.shape[1]

    def kernel(body, name, outs, specs, scratch, mib, work):
        return pl.pallas_call(
            body,
            name=name,
            out_shape=tuple(outs),
            in_specs=specs,
            out_specs=(IN_VMEM,) * len(outs),
            scratch_shapes=scratch,
            compiler_params=pltpu.CompilerParams(vmem_limit_bytes=mib * MIB),
            cost_estimate=pl.CostEstimate(
                flops=2 * tok_rows * width * work, bytes_accessed=mib * MIB, transcendentals=0
            ),
        )

    seqs_shape = pltpu.VMEM((seq_dev, pad_rows, width), jnp.float32)
    codes_shape = pltpu.VMEM((SUBLANES, LANES), jnp.float32)
    score_shape = pltpu.VMEM((seq_dev * loop_count, LANES), jnp.float32)
    tiles = (tok_rows // SUBLANES) * (width // LANES) + 1
    message_shape = pltpu.VMEM((tiles, SUBLANES, LANES), jnp.int16)

    def to_pair(out, step):
        pairs = [
            (source * loop_count + core, (source ^ (1 << (core ^ step))) * loop_count + core)
            for source in range(layer_count)
            for core in range(loop_count)
        ]
        return in_vmem(lax.ppermute(out, both, pairs))

    other_act = from_partner(act_factors, "loop", 1)
    own_total, own_out, act_held, factor_held = kernel(
        act_own_kernel, "act_own_columns",
        (
            seqs_shape, message_shape, pltpu.VMEM(acts.shape, acts.dtype),
            pltpu.VMEM(grad_factors.shape, grad_factors.dtype),
        ),
        [IN_HBM] * 3,
        [pltpu.VMEM(act_factors.shape, act_factors.dtype), codes_shape, pltpu.SemaphoreType.DMA((6,))],
        ACT_OWN_MIB, acts.shape[1],
    )(in_hbm(acts), in_hbm(act_factors), in_hbm(grad_factors))
    own_in = to_pair(own_out, 1 - GRAD_STEP)
    later_factors, other_act, own_total = lax.optimization_barrier((grad_factors, other_act, own_total))
    other_grad = from_partner(later_factors, "loop", 1)
    other_total, other_out = kernel(
        act_other_kernel, "act_other_columns", (seqs_shape, message_shape), [IN_VMEM] * 2, [codes_shape],
        8, acts.shape[1],
    )(in_vmem(act_held), in_vmem(other_act))
    other_in = to_pair(other_out, 0)
    grad_own, grad_out = kernel(
        grad_own_kernel, "grad_own_columns", (seqs_shape, message_shape), [IN_VMEM] * 2, [codes_shape], 16, depth,
    )(in_vmem(grads), in_vmem(factor_held))
    grad_in = to_pair(grad_out, GRAD_STEP)
    other_pair, other_out = kernel(
        pair_kernel, "other_pair", (seqs_shape, message_shape), [IN_VMEM] * 3, [codes_shape], 8, 0,
    )(in_vmem(other_total), other_in, in_vmem(grad_own))
    other_in = to_pair(other_out, 1)
    (grad_other,) = kernel(
        grad_other_kernel, "grad_other_columns", (seqs_shape,), [IN_VMEM] * 2, [], 16, depth,
    )(in_vmem(grads), in_vmem(other_grad))
    own_scores, grad_other = kernel(
        own_score_kernel, "own_scores", (score_shape, seqs_shape), [IN_SMEM] + [IN_VMEM] * 5, [seqs_shape] * 2, 8, 0,
    )(lengths, in_vmem(own_total), own_in, in_vmem(grad_own), grad_in, in_vmem(grad_other))
    (total,) = kernel(
        other_score_kernel, "other_scores", (score_shape,), [IN_VMEM] * 4, [seqs_shape], 8, 0,
    )(in_vmem(other_pair), other_in, in_vmem(grad_other), in_vmem(own_scores))

    total = total + from_partner(total, "loop", 1)
    gathered = [from_partner(total, both, mask * loop_count + 1) for mask in range(1, QUARTERS)]
    total = total + gathered[0] + gathered[1] + gathered[2]
    mask = QUARTERS
    while mask < layer_count:
        total = total + from_partner(total, both, mask * loop_count + 1)
        mask *= 2
    return total[:, :queries]


def solution(mesh):
    in_specs = (
        P("layer", ("groups", "loop"), None),
        P("layer", ("groups", "loop"), None),
        P("layer", None, "loop"),
        P("layer", None, "loop"),
        P(("groups", "loop")),
    )
    out_specs = P("groups", None)
    return jax.shard_map(
        on_device, mesh=mesh, in_specs=in_specs, out_specs=out_specs, check_vma=False
    )
```
